256 devices in a mesh: tp: 8 (over y, core), row: 4 (over x), kv: 8 (over z).
Axes of the slice: x: 4, y: 4, z: 8, core: 2. Of those that a mesh axis runs over, the one named last changes fastest.
Arguments:
- tokens: bfloat16 [32, 8192], P(None, ('row', 'kv')), may hold values from -5 to 5
- attn_gain: bfloat16 [8192], P(('row', 'kv')), may hold values from 0.099609375 to 1.8984375
- w_qkv: bfloat16 [8192, 10240], P(('row', 'kv'), 'tp'), may hold values from -0.0625 to 0.0625
- w_out: bfloat16 [8192, 8192], P('tp', ('row', 'kv')), may hold values from -0.0625 to 0.0625
- ffn_gain: bfloat16 [8192], P(('row', 'kv')), may hold values from 0.099609375 to 1.8984375
- w_gate: bfloat16 [8192, 14336], P(('row', 'kv'), 'tp'), may hold values from -0.0625 to 0.0625
- w_up: bfloat16 [8192, 14336], P(('row', 'kv'), 'tp'), may hold values from -0.0625 to 0.0625
- w_down: bfloat16 [14336, 8192], P('tp', ('row', 'kv')), may hold values from -0.09375 to 0.09375
- cache_keys: bfloat16 [32, 16384, 1024], P('row', 'kv', 'tp'), may hold values from -94 to 94
- cache_values: bfloat16 [32, 16384, 1024], P('row', 'kv', 'tp'), may hold values from -10 to 10
- cache_len: int32 [32], replicated, may hold values from 1 to 16383, 209715 in all
- pool_seq: int32 [32], replicated, may hold values from 0 to 31, each once
Outputs:
- layer_out: bfloat16 [32, 8192], P(None, ('row', 'kv'))
- new_keys: bfloat16 [32, 1024], P('row', 'tp')
- new_values: bfloat16 [32, 1024], P('row', 'tp')
The draws below stay inside these ranges and needn't reach their ends.
Inputs may be any that keep to these rules, and one draw needn't show every extreme that they name: `cache_len`: cache lengths of the sequences; they sum to 209715 and the largest is exactly 16383. `pool_seq`: each sequence stands in exactly one pool slot.
All inputs are finite; a program needn't handle non-finite values.
Results may differ from the reference program's by a relative error of at most 0.02.
Values may be sent and summed in bfloat16 or wider, within the bound.
A program may use at most 64 MiB of HBM per device.

```python
import math
import jax
import jax.numpy as jnp
import numpy as np
from jax import lax

D = 8192
HEADS = 64
KV_HEADS = 8
HEAD = 128
FF_WIN = 14336
GROUP = 8
SEQS = 32
LMAX = 16384


def draw_tokens(key, part):
    key = jax.random.fold_in(key, 13)
    noise_part = jnp.clip(jax.random.normal(jax.random.fold_in(key, 1), (SEQS, D), jnp.float32), -4.0, 4.0)
    row_scale = jnp.exp(jax.random.uniform(jax.random.fold_in(key, 2), (SEQS, 1), jnp.float32, 0.0, math.log(10.0)))
    rising = 3.0
    column_pos = jnp.arange(D, dtype=jnp.float32)[None, :] / D
    column_spread = jax.random.uniform(jax.random.fold_in(key, 3), (1, D), jnp.float32, 0.0, math.log(10.0 / rising))
    column_scale = jnp.exp(column_pos * math.log(rising) + column_spread)
    return (noise_part * row_scale * column_scale * 0.0125).astype(jnp.bfloat16)


def draw_cache_keys(key, part):
    key = jax.random.fold_in(key, 17)
    shape_all = (SEQS, LMAX, KV_HEADS * HEAD)
    strong_pick = jax.random.uniform(jax.random.fold_in(key, 2), (SEQS, LMAX, 1), jnp.float32) < 0.02
    strong_level = jax.random.uniform(jax.random.fold_in(key, 3), (SEQS, LMAX, 1), jnp.float32, 35.0, 55.0)
    base_part = jax.random.normal(jax.random.fold_in(key, 1), shape_all, jnp.float32)
    strong_part = jnp.clip(base_part, -1.7, 1.7) * strong_level
    return jnp.where(strong_pick, strong_part, jnp.clip(base_part, -6.0, 6.0)).astype(jnp.bfloat16)


def draw_cache_values(key, part):
    key = jax.random.fold_in(key, 19)
    channel_count = KV_HEADS * HEAD
    noise_part = jnp.clip(jax.random.normal(jax.random.fold_in(key, 1), (SEQS, LMAX, channel_count), jnp.float32), -5.0, 5.0)
    level_part = jnp.clip(jax.random.normal(jax.random.fold_in(key, 2), (SEQS, LMAX // 32, 1, channel_count), jnp.float32), -3.0, 3.0)
    level_part = jnp.broadcast_to(level_part, (SEQS, LMAX // 32, 32, channel_count)).reshape(SEQS, LMAX, channel_count)
    return (noise_part + 1.5 * level_part).astype(jnp.bfloat16)


def level_of(rng, dims, pieces, smallest, top_value):
    factor_of = 1.0
    for dim, blocks in pieces:
        heights = jax.random.uniform(jax.random.fold_in(jax.random.fold_in(rng, 6), dim), (blocks,), jnp.float32, smallest / len(pieces), top_value / len(pieces))
        factor_of = factor_of * jnp.repeat(jnp.exp(heights), dims[dim] // blocks).reshape((-1,) + (1,) * (len(dims) - 1 - dim))
    return factor_of


def length_profile(amount, total, bound, lean):
    loads = [(1 << 20) // math.isqrt(standing ** lean) + 1 for standing in range(2, amount + 1)]
    surplus, given = total - bound - (amount - 1), [1] * (amount - 1)
    while surplus > 0:
        candidates = [i for i in range(amount - 1) if given[i] < bound]
        mass, remaining = sum([loads[i] for i in candidates]), surplus
        for i in candidates:
            more = min(bound - given[i], max(1, remaining * loads[i] // mass), surplus)
            given[i] = given[i] + more
            surplus = surplus - more
    return np.array([bound] + given)


def uneven_parts(key, count, total, bound, slope):
    if count == 2:
        one = jax.random.randint(key, (), max(1, total - bound), min(bound, total - 1) + 1)
        return jnp.stack([one, total - one])
    tallies = jnp.asarray(length_profile(count, total, bound, slope), jnp.int32)
    pairs = (count - 1) // 2
    giver, taker = tallies[1:1 + 2 * pairs:2], tallies[2:2 + 2 * pairs:2]
    room = jnp.minimum(giver - 1, bound - taker)
    shifted = jax.random.randint(jax.random.fold_in(key, 1), (pairs,), 0, 1 << 20) % (room + 1)
    tallies = tallies.at[1:1 + 2 * pairs:2].set(giver - shifted).at[2:2 + 2 * pairs:2].set(taker + shifted)
    return tallies[jax.random.permutation(jax.random.fold_in(key, 2), count)]


def normal_values(stream_key, shape, deviation, most, cuts=(), held_as=jnp.bfloat16):
    array = jax.random.normal(stream_key, shape, jnp.float32) * deviation
    if len(cuts) > 0:
        array = level_of(stream_key, shape, cuts, -0.22, 0.18) * array
    return jnp.clip(array, min=-most, max=most).astype(held_as)


def setup_inputs(seed: int = 0) -> dict:
    arg_keys = jax.random.split(jax.random.key(seed), 13)
    return {
        "tokens": draw_tokens(jax.random.fold_in(arg_keys[12], 71), 0),
        "attn_gain": jnp.clip(1.0 + 0.18 * jax.random.normal(arg_keys[1], (D,), jnp.float32), 0.099609375, 1.8984375).astype(jnp.bfloat16),
        "w_qkv": normal_values(arg_keys[2], (D, KV_HEADS * (GROUP + 2) * HEAD), D ** -0.5, 0.0625, ((0, 32), (1, 8))),
        "w_out": normal_values(arg_keys[3], (HEADS * HEAD, D), (HEADS * HEAD) ** -0.5, 0.0625, ((0, 8), (1, 32))),
        "ffn_gain": jnp.clip(1.0 + 0.18 * jax.random.normal(arg_keys[4], (D,), jnp.float32), 0.099609375, 1.8984375).astype(jnp.bfloat16),
        "w_gate": normal_values(arg_keys[5], (D, FF_WIN), D ** -0.5, 0.0625, ((0, 32), (1, 8))),
        "w_up": normal_values(arg_keys[6], (D, FF_WIN), D ** -0.5, 0.0625, ((0, 32), (1, 8))),
        "w_down": normal_values(arg_keys[7], (FF_WIN, D), (FF_WIN // 4) ** -0.5, 0.09375, ((0, 8), (1, 32))),
        "cache_keys": draw_cache_keys(jax.random.fold_in(arg_keys[12], 71), 0),
        "cache_values": draw_cache_values(jax.random.fold_in(arg_keys[12], 71), 0),
        "cache_len": uneven_parts(arg_keys[10], SEQS, SEQS * LMAX * 2 // 5, LMAX - 1, 2).astype(jnp.int32),
        "pool_seq": jax.random.permutation(arg_keys[11], SEQS).astype(jnp.int32),
    }


epsilon = 1e-05
rope_base = 500000.0
floor_score = -1e+30

def rotate(vectors, positions):
    half_width = vectors.shape[-1] // 2
    frequency = rope_base ** (-(jnp.arange(half_width, dtype=jnp.float32) * 2.0 / vectors.shape[-1]))
    angles = positions.astype(jnp.float32)[:, None] * frequency[None, :]
    cosine = jnp.cos(angles)[:, None, :]
    sine_part = jnp.sin(angles)[:, None, :]
    first_half = vectors[..., :half_width]
    second_half = vectors[..., half_width:]
    return jnp.concatenate([first_half * cosine - second_half * sine_part, second_half * cosine + first_half * sine_part], axis=-1)

def norm_rows(values, gain):
    mean_square = lax.optimization_barrier(jnp.sum(values * values, axis=1)) / D
    return (values * lax.rsqrt(mean_square + epsilon)[:, None] * gain.astype(jnp.float32)).astype(jnp.bfloat16)

def attend_slot(items):
    slot_keys, slot_values, slot_query, fresh_key, fresh_value, length_now = items
    score_scale = HEAD ** (-0.5)
    keys_wide = slot_keys.astype(jnp.float32).reshape(LMAX, KV_HEADS, HEAD)
    values_wide = slot_values.astype(jnp.float32).reshape(LMAX, KV_HEADS, HEAD)
    grouped = slot_query.astype(jnp.float32).reshape(KV_HEADS, GROUP, HEAD)
    cache_scores = jnp.einsum('kgd,tkd->kgt', grouped, keys_wide) * score_scale
    fresh_scores = jnp.einsum('kgd,kd->kg', grouped, fresh_key.astype(jnp.float32))[..., None] * score_scale
    allowed = jnp.arange(LMAX) < length_now
    allowed_all = jnp.concatenate([allowed, jnp.ones((1,), bool)])
    scores = jnp.concatenate([jnp.where(allowed, cache_scores, floor_score), fresh_scores], axis=-1)
    peak_score = lax.optimization_barrier(jnp.max(scores, axis=-1, keepdims=True))
    weights = jnp.where(allowed_all, jnp.exp(scores - peak_score), 0.0)
    weight_sum = lax.optimization_barrier(jnp.sum(weights, axis=-1))
    rounded_weights = lax.optimization_barrier(weights.astype(jnp.bfloat16)).astype(jnp.float32)
    all_values = jnp.concatenate([values_wide, fresh_value.astype(jnp.float32)[None]], axis=0)
    numerator = jnp.einsum('kgt,tkd->kgd', rounded_weights, all_values)
    return (numerator / weight_sum[..., None]).astype(jnp.bfloat16).reshape(HEADS * HEAD)

def reference(tokens, attn_gain, w_qkv, w_out, ffn_gain, w_gate, w_up, w_down, cache_keys, cache_values, cache_len, pool_seq):
    stream = tokens.astype(jnp.float32)
    normed = norm_rows(stream, attn_gain)
    ordered = normed[pool_seq]
    united_rows = jnp.dot(ordered, w_qkv, preferred_element_type=jnp.float32).reshape(SEQS, KV_HEADS, GROUP + 2, HEAD)
    limits = cache_len[pool_seq]
    queries = rotate(united_rows[:, :, :GROUP].reshape(SEQS, HEADS, HEAD), limits).astype(jnp.bfloat16)
    key_new = rotate(united_rows[:, :, GROUP], limits).astype(jnp.bfloat16)
    value_new = united_rows[:, :, GROUP + 1].astype(jnp.bfloat16)
    mixed = lax.map(attend_slot, (cache_keys, cache_values, queries, key_new, value_new, limits))
    slot_of = jnp.zeros((SEQS,), jnp.int32).at[pool_seq].set(jnp.arange(SEQS, dtype=jnp.int32))
    projected = jnp.dot(mixed[slot_of], w_out, preferred_element_type=jnp.float32)
    stream_two = (stream + projected).astype(jnp.bfloat16)
    normed_two = norm_rows(stream_two.astype(jnp.float32), ffn_gain)
    gate_sum = jnp.dot(normed_two, w_gate, preferred_element_type=jnp.float32)
    up_sum = jnp.dot(normed_two, w_up, preferred_element_type=jnp.float32)
    activated = (jax.nn.silu(gate_sum) * up_sum).astype(jnp.bfloat16)
    down_sum = jnp.dot(activated, w_down, preferred_element_type=jnp.float32)
    layer_out = (stream_two.astype(jnp.float32) + down_sum).astype(jnp.bfloat16)
    return (layer_out, key_new.reshape(SEQS, KV_HEADS * HEAD), value_new.reshape(SEQS, KV_HEADS * HEAD))
```

```python
import functools

import jax
import jax.numpy as jnp
from jax import lax
from jax.experimental import pallas as pl
from jax.experimental.pallas import tpu as pltpu
from jax.sharding import PartitionSpec as P

D = 8192
HEAD = 128
GROUP = 8
EPSILON = 1e-05
ROPE_BASE = 500000.0
FLOOR = -1e30
MESH = pl.DeviceIdType.MESH
F32 = jnp.float32
BF16 = jnp.bfloat16


def iota(shape, dim):
    return lax.broadcasted_iota(jnp.int32, shape, dim)


def kernel(
    tp_size,
    row_size,
    kv_size,
    pool_smem,
    len_smem,
    pool_row,
    tokens,
    gains,
    cosines,
    sines,
    w_qkv,
    w_out,
    w_gate,
    w_up,
    w_down,
    cache_keys,
    cache_values,
    layer_out,
    new_keys,
    new_values,
    qkv_v,
    out_v,
    gate_v,
    up_v,
    down_v,
    keys_v,
    values_v,
    s1,
    r1,
    s2,
    r2,
    s3,
    r3,
    s4,
    r4,
    s5,
    r5,
    s6,
    r6,
    w7,
    s7,
    r7,
    s8,
    r8,
    w8,
    s9,
    r9,
    load_sems,
    send_sems,
    recv_sems,
):
    plane = row_size * kv_size
    tp = lax.axis_index("tp")
    row = lax.axis_index("row")
    kv = lax.axis_index("kv")
    me = row * kv_size + kv

    barrier = pltpu.get_barrier_semaphore()

    def greet_plane(step, carry):
        other = lax.rem(me + step, plane)
        pl.semaphore_signal(
            barrier,
            inc=1,
            device_id={"row": other // kv_size, "kv": lax.rem(other, kv_size)},
            device_id_type=MESH,
        )
        return carry

    def greet_tp(step, carry):
        pl.semaphore_signal(
            barrier, inc=1, device_id={"tp": lax.rem(tp + step, tp_size)}, device_id_type=MESH
        )
        return carry

    lax.fori_loop(1, plane, greet_plane, 0)
    lax.fori_loop(1, tp_size, greet_tp, 0)

    loads = []
    for index, (source, target) in enumerate(
        (
            (w_qkv, qkv_v),
            (cache_keys, keys_v),
            (cache_values, values_v),
            (w_out, out_v),
            (w_gate, gate_v),
            (w_up, up_v),
            (w_down, down_v),
        )
    ):
        load = pltpu.make_async_copy(source, target, load_sems.at[index])
        load.start()
        loads.append(load)

    def send_plane(phase, source, target):
        def one(step, carry):
            other = lax.rem(me + step, plane)
            pltpu.make_async_remote_copy(
                src_ref=source(other),
                dst_ref=target,
                send_sem=send_sems.at[phase],
                recv_sem=recv_sems.at[phase],
                device_id={"row": other // kv_size, "kv": lax.rem(other, kv_size)},
                device_id_type=MESH,
            ).start()
            return carry

        lax.fori_loop(1, plane, one, 0)

    def send_kv(phase, source, target):
        def one(step, carry):
            other = lax.rem(kv + step, kv_size)
            pltpu.make_async_remote_copy(
                src_ref=source(other),
                dst_ref=target,
                send_sem=send_sems.at[phase],
                recv_sem=recv_sems.at[phase],
                device_id={"kv": other},
                device_id_type=MESH,
            ).start()
            return carry

        lax.fori_loop(1, kv_size, one, 0)

    def send_tp(phase, source, target):
        def one(step, carry):
            pltpu.make_async_remote_copy(
                src_ref=source,
                dst_ref=target,
                send_sem=send_sems.at[phase],
                recv_sem=recv_sems.at[phase],
                device_id={"tp": lax.rem(tp + step, tp_size)},
                device_id_type=MESH,
            ).start()
            return carry

        lax.fori_loop(1, tp_size, one, 0)

    def whole(phase, part):
        return pltpu.make_async_remote_copy(
            src_ref=part,
            dst_ref=part,
            send_sem=send_sems.at[phase],
            recv_sem=recv_sems.at[phase],
            device_id={"tp": tp},
            device_id_type=MESH,
        )

    others = {
        0: r1.at[pl.ds(0, plane - 1)],
        1: r2.at[pl.ds(0, plane - 1)],
        2: r3.at[pl.ds(0, kv_size - 1)],
        3: r4.at[pl.ds(0, kv_size - 1)],
        4: r5.at[pl.ds(0, (plane - 1) * 8)],
        5: r6.at[pl.ds(0, tp_size - 1)],
        6: r7.at[pl.ds(0, plane - 1)],
        7: r8.at[pl.ds(0, plane - 1)],
        8: r9.at[pl.ds(0, tp_size - 1)],
    }

    def arrived(phase):
        whole(phase, others[phase]).wait_recv()

    seqs = tokens.shape[0]
    width = tokens.shape[1]
    pool_lane = pool_row[...]
    diagonal = iota((seqs, seqs), 0) == iota((seqs, seqs), 1)
    spread = jnp.broadcast_to(pool_lane, (seqs, seqs))
    pool_column = jnp.sum(jnp.where(diagonal, spread, 0), axis=1, keepdims=True)
    to_slots = (pool_column == iota((seqs, seqs), 1)).astype(BF16)
    to_seqs = (spread == iota((seqs, seqs), 0)).astype(BF16)
    stream = jnp.dot(to_slots, tokens[...], preferred_element_type=F32)

    wide = iota((seqs, HEAD), 0) == iota((seqs, HEAD), 1)

    def as_lanes(column):
        return jnp.sum(
            jnp.where(wide, jnp.broadcast_to(column, (seqs, HEAD)), 0.0), axis=0, keepdims=True
        )

    def as_column(lanes):
        return jnp.sum(
            jnp.where(wide, jnp.broadcast_to(lanes, (seqs, HEAD)), 0.0), axis=1, keepdims=True
        )

    squares = as_lanes(jnp.sum(stream * stream, axis=1, keepdims=True))
    s1[0] = squares
    r1[me] = squares

    pl.semaphore_wait(barrier, plane - 1 + tp_size - 1)

    send_plane(0, lambda other: s1.at[0], r1.at[me])
    blank = jnp.zeros((seqs, HEAD), F32)
    for part in range(GROUP + 2, 16):
        s2[pl.ds(part, seqs, stride=16), :] = blank
    arrived(0)
    first_sum = as_column(jnp.sum(r1[...], axis=0))
    normed = (stream * lax.rsqrt(first_sum / D + EPSILON) * gains[0:1, :]).astype(BF16)

    loads[0].wait()
    united = jnp.dot(normed, qkv_v[...], preferred_element_type=F32)
    for part in range(GROUP + 2):
        s2[pl.ds(part, seqs, stride=16), :] = united[:, part * HEAD : (part + 1) * HEAD]
    send_plane(1, lambda other: s2.at[pl.ds(pl.multiple_of(other * 16, 16), 16), :], r2.at[me])
    r2[me] = s2[pl.ds(pl.multiple_of(me * 16, 16), 16), :]
    my_seq = pool_smem[me]
    pick = iota((seqs, HEAD), 0) == my_seq
    cosine = jnp.sum(jnp.where(pick, cosines[...], 0.0), axis=0, keepdims=True)
    sine = jnp.sum(jnp.where(pick, sines[...], 0.0), axis=0, keepdims=True)
    rotated = iota((16, HEAD), 0) <= GROUP
    cosine = jnp.where(rotated, jnp.broadcast_to(cosine, (16, HEAD)), 1.0)
    sine = jnp.where(rotated, jnp.broadcast_to(sine, (16, HEAD)), 0.0)
    arrived(1)
    mine = jnp.sum(r2[...], axis=0)
    mine = mine * cosine + pltpu.roll(mine, HEAD // 2, 1) * sine
    mine = mine.astype(BF16)

    s3[...] = mine
    r3[kv] = mine
    send_kv(2, lambda other: s3, r3.at[kv])
    fresh_query = mine[:GROUP].astype(F32)
    fresh_key = mine[GROUP : GROUP + 1].astype(F32)
    fresh_value = mine[GROUP + 1 : GROUP + 2].astype(F32)
    score_scale = HEAD ** (-0.5)
    fresh_score = jnp.sum(fresh_query * fresh_key, axis=1, keepdims=True) * score_scale
    loads[1].wait()
    loads[2].wait()
    arrived(2)
    slots = r3.shape[0]
    rows_now = r3[...].astype(F32)
    new_keys[...] = jnp.concatenate(
        [rows_now[slot, GROUP : GROUP + 1] for slot in range(slots)], axis=0
    ).astype(BF16)
    new_values[...] = jnp.concatenate(
        [rows_now[slot, GROUP + 1 : GROUP + 2] for slot in range(slots)], axis=0
    ).astype(BF16)

    block = keys_v.shape[1]
    position = kv * block + iota((GROUP, block), 1)
    lane = iota((GROUP, HEAD), 1)
    for slot in range(slots):
        limit = len_smem[pool_smem[row * slots + slot]]
        scores = (
            lax.dot_general(
                r3[slot, :GROUP, :],
                keys_v[slot],
                (((1,), (1,)), ((), ())),
                preferred_element_type=F32,
            )
            * score_scale
        )
        allowed = position < limit
        peak = jnp.max(jnp.where(allowed, scores, FLOOR), axis=1, keepdims=True)
        weights = jnp.where(allowed, jnp.exp(scores - peak), 0.0)
        total = jnp.sum(weights, axis=1, keepdims=True)
        product = jnp.dot(weights.astype(BF16), values_v[slot], preferred_element_type=F32)
        s4[slot * 16 : slot * 16 + GROUP, :] = product
        s4[slot * 16 + GROUP : slot * 16 + 16, :] = jnp.where(lane == 0, peak, total)

    send_kv(3, lambda other: s4.at[pl.ds(pl.multiple_of(other * 16, 16), 16), :], r4.at[kv])
    r4[kv] = s4[pl.ds(pl.multiple_of(kv * 16, 16), 16), :]
    arrived(3)
    parts = r4[...]
    peaks = [parts[source, GROUP:, 0:1] for source in range(slots)]
    joint = fresh_score
    for peak in peaks:
        joint = jnp.maximum(joint, peak)
    fresh_weight = jnp.exp(fresh_score - joint)
    total = fresh_weight
    numer = fresh_weight.astype(BF16).astype(F32) * fresh_value
    for source in range(slots):
        fade = jnp.exp(peaks[source] - joint)
        total = total + parts[source, GROUP:, 1:2] * fade
        numer = numer + parts[source, :GROUP] * fade
    mixed = numer / total

    s5[...] = mixed
    r5[pl.ds(pl.multiple_of(me * 8, 8), 8), :] = mixed
    send_plane(4, lambda other: s5, r5.at[pl.ds(pl.multiple_of(me * 8, 8), 8), :])
    loads[3].wait()
    arrived(4)
    mixed_all = jnp.concatenate(
        [r5[pl.ds(head, seqs, stride=8), :].astype(BF16) for head in range(GROUP)], axis=1
    )
    projected = jnp.dot(mixed_all, out_v[...], preferred_element_type=F32)

    s6[...] = projected
    r6[tp] = projected
    send_tp(5, s6, r6.at[tp])
    loads[4].wait()
    loads[5].wait()
    arrived(5)
    projected = r6[0]
    for source in range(1, tp_size):
        projected = projected + r6[source]
    stream_two = (stream + projected).astype(BF16).astype(F32)
    square_column = jnp.broadcast_to(
        jnp.sum(stream_two * stream_two, axis=1, keepdims=True), (seqs, HEAD)
    )
    scaled = (stream_two * gains[1:2, :]).astype(BF16)

    gate = jnp.dot(scaled, gate_v[...], preferred_element_type=F32)
    up = jnp.dot(scaled, up_v[...], preferred_element_type=F32)
    chunks = gate.shape[1] // HEAD
    for part in range(chunks):
        w7[pl.ds(part, seqs, stride=32), :] = gate[:, part * HEAD : (part + 1) * HEAD]
        w7[pl.ds(part + 16, seqs, stride=32), :] = up[:, part * HEAD : (part + 1) * HEAD]
    high = square_column.astype(BF16).astype(F32)
    w7[pl.ds(14, seqs, stride=32), :] = high
    w7[pl.ds(15, seqs, stride=32), :] = square_column - high
    w7[pl.ds(30, seqs, stride=32), :] = blank
    w7[pl.ds(31, seqs, stride=32), :] = blank
    s7[...] = w7[...].astype(BF16)
    send_plane(6, lambda other: s7.at[pl.ds(pl.multiple_of(other * 32, 32), 32), :], r7.at[me])
    r7[me] = s7[pl.ds(pl.multiple_of(me * 32, 32), 32), :]
    loads[6].wait()
    arrived(6)
    sums = jnp.sum(r7[...].astype(F32), axis=0)
    scale = lax.rsqrt((sums[14:15] + sums[15:16]) / D + EPSILON)
    gate = sums[:16] * scale
    up = sums[16:] * scale
    activated = (gate / (1.0 + jnp.exp(-gate)) * up).astype(BF16)

    s8[...] = activated
    r8[me] = activated
    send_plane(7, lambda other: s8, r8.at[me])
    arrived(7)
    w8[...] = r8[...].astype(F32).reshape(w8.shape)
    active_all = jnp.concatenate(
        [w8[pl.ds(part, seqs, stride=16), :].astype(BF16) for part in range(chunks)], axis=1
    )
    down = jnp.dot(active_all, down_v[...], preferred_element_type=F32)

    s9[...] = down
    r9[tp] = down
    send_tp(8, s9, r9.at[tp])
    arrived(8)
    down = r9[0]
    for source in range(1, tp_size):
        down = down + r9[source]
    result = (stream_two + down).astype(BF16)
    layer_out[...] = jnp.dot(to_seqs, result, preferred_element_type=F32).astype(BF16)

    for phase in range(9):
        whole(phase, others[phase]).wait_send()


def local(
    sizes,
    tokens,
    attn_gain,
    w_qkv,
    w_out,
    ffn_gain,
    w_gate,
    w_up,
    w_down,
    cache_keys,
    cache_values,
    cache_len,
    pool_seq,
):
    tp_size, row_size, kv_size = sizes
    seqs, width = tokens.shape
    half = HEAD // 2
    frequency = ROPE_BASE ** (-(jnp.arange(half, dtype=F32) * 2.0 / HEAD))
    angles = cache_len.astype(F32)[:, None] * frequency[None, :]
    cosine = jnp.cos(angles)
    sine = jnp.sin(angles)
    cosines = jnp.concatenate([cosine, cosine], axis=1)
    sines = jnp.concatenate([-sine, sine], axis=1)
    gains = jnp.stack([attn_gain.astype(F32), ffn_gain.astype(F32)])
    plane = row_size * kv_size
    vmem = pl.BlockSpec(memory_space=pltpu.VMEM)
    smem = pl.BlockSpec(memory_space=pltpu.SMEM)
    hbm = pl.BlockSpec(memory_space=pl.ANY)
    scratch = [
        pltpu.VMEM(w_qkv.shape, BF16),
        pltpu.VMEM(w_out.shape, BF16),
        pltpu.VMEM(w_gate.shape, BF16),
        pltpu.VMEM(w_up.shape, BF16),
        pltpu.VMEM(w_down.shape, BF16),
        pltpu.VMEM(cache_keys.shape, BF16),
        pltpu.VMEM(cache_values.shape, BF16),
        pltpu.VMEM((1, 1, HEAD), F32),
        pltpu.VMEM((plane, 1, HEAD), F32),
        pltpu.VMEM((plane * 16, HEAD), F32),
        pltpu.VMEM((plane, 16, HEAD), F32),
        pltpu.VMEM((16, HEAD), BF16),
        pltpu.VMEM((kv_size, 16, HEAD), BF16),
        pltpu.VMEM((kv_size * 16, HEAD), F32),
        pltpu.VMEM((kv_size, 16, HEAD), F32),
        pltpu.VMEM((8, HEAD), F32),
        pltpu.VMEM((plane * 8, HEAD), F32),
        pltpu.VMEM((seqs, width), F32),
        pltpu.VMEM((tp_size, seqs, width), F32),
        pltpu.VMEM((plane * 32, HEAD), F32),
        pltpu.VMEM((plane * 32, HEAD), BF16),
        pltpu.VMEM((plane, 32, HEAD), BF16),
        pltpu.VMEM((16, HEAD), BF16),
        pltpu.VMEM((plane, 16, HEAD), BF16),
        pltpu.VMEM((plane * 16, HEAD), F32),
        pltpu.VMEM((seqs, width), F32),
        pltpu.VMEM((tp_size, seqs, width), F32),
        pltpu.SemaphoreType.DMA((7,)),
        pltpu.SemaphoreType.DMA((9,)),
        pltpu.SemaphoreType.DMA((9,)),
    ]
    return pl.pallas_call(
        functools.partial(kernel, tp_size, row_size, kv_size),
        out_shape=(
            jax.ShapeDtypeStruct((seqs, width), BF16),
            jax.ShapeDtypeStruct((kv_size, HEAD), BF16),
            jax.ShapeDtypeStruct((kv_size, HEAD), BF16),
        ),
        in_specs=[smem, smem] + [vmem] * 5 + [hbm] * 7,
        out_specs=(vmem, vmem, vmem),
        scratch_shapes=scratch,
        compiler_params=pltpu.CompilerParams(
            collective_id=0, has_side_effects=True, vmem_limit_bytes=40 * 1024 * 1024
        ),
    )(
        pool_seq,
        cache_len,
        pool_seq.reshape(1, -1),
        tokens,
        gains,
        cosines,
        sines,
        w_qkv,
        w_out,
        w_gate,
        w_up,
        w_down,
        cache_keys,
        cache_values,
    )


def solution(mesh):
    sizes = (mesh.shape["tp"], mesh.shape["row"], mesh.shape["kv"])
    return jax.shard_map(
        functools.partial(local, sizes),
        mesh=mesh,
        in_specs=(
            P(None, ("row", "kv")),
            P(("row", "kv")),
            P(("row", "kv"), "tp"),
            P("tp", ("row", "kv")),
            P(("row", "kv")),
            P(("row", "kv"), "tp"),
            P(("row", "kv"), "tp"),
            P("tp", ("row", "kv")),
            P("row", "kv", "tp"),
            P("row", "kv", "tp"),
            P(),
            P(),
        ),
        out_specs=(P(None, ("row", "kv")), P("row", "tp"), P("row", "tp")),
        check_vma=False,
    )
```

```python
import functools

import jax
import jax.numpy as jnp
from jax import lax
from jax.experimental import pallas as pl
from jax.experimental.pallas import tpu as pltpu
from jax.sharding import PartitionSpec as P

D = 8192
HEAD = 128
GROUP = 8
EPSILON = 1e-05
ROPE_BASE = 500000.0
FLOOR = -1e30
MESH = pl.DeviceIdType.MESH
F32 = jnp.float32
BF16 = jnp.bfloat16


def iota(shape, dim):
    return lax.broadcasted_iota(jnp.int32, shape, dim)


def far_first(index, size):
    half = (index + 1) // 2
    return size // 2 + (1 - 2 * lax.rem(index, 2)) * half


def kernel(
    tp_size,
    row_size,
    kv_size,
    frequency_hbm,
    pool_hbm,
    len_hbm,
    tokens_hbm,
    attn_hbm,
    ffn_hbm,
    w_qkv,
    w_out,
    w_gate,
    w_up,
    w_down,
    cache_keys,
    cache_values,
    layer_out,
    new_keys,
    new_values,
    frequency,
    pool_smem,
    len_smem,
    tokens,
    attn_gain,
    ffn_gain,
    qkv_v,
    out_v,
    gate_v,
    up_v,
    down_v,
    keys_v,
    values_v,
    s1,
    r1,
    s2,
    r2,
    sf,
    rf,
    s3,
    r3,
    sp,
    rp,
    s4,
    r4,
    s5,
    r5,
    s6,
    r6,
    w7,
    s7,
    r7,
    s8,
    r8,
    w8,
    s9,
    r9,
    s_out,
    load_sems,
    send_sems,
    recv_sems,
    query_sems,
    out_sems,
):
    plane = row_size * kv_size
    tp = lax.axis_index("tp")
    row = lax.axis_index("row")
    kv = lax.axis_index("kv")
    me = row * kv_size + kv

    barrier = pltpu.get_barrier_semaphore()

    def plane_partner(index):
        other_row = lax.rem(row + far_first(lax.rem(index, row_size), row_size), row_size)
        other_kv = lax.rem(kv + far_first(index // row_size, kv_size), kv_size)
        return other_row, other_kv

    def greet_plane(index, carry):
        other_row, other_kv = plane_partner(index)
        pl.semaphore_signal(
            barrier,
            inc=1,
            device_id={"row": other_row, "kv": other_kv},
            device_id_type=MESH,
        )
        return carry

    def greet_tp(step, carry):
        pl.semaphore_signal(
            barrier, inc=1, device_id={"tp": lax.rem(tp + step, tp_size)}, device_id_type=MESH
        )
        return carry

    lax.fori_loop(0, plane - 1, greet_plane, 0)
    lax.fori_loop(1, tp_size, greet_tp, 0)

    pending = {}
    for index, (name, source, target) in enumerate(
        (
            ("pool", pool_hbm, pool_smem),
            ("tokens", tokens_hbm, tokens),
            ("len", len_hbm, len_smem),
            ("attn", attn_hbm, attn_gain),
            ("frequency", frequency_hbm, frequency),
            ("qkv", w_qkv, qkv_v),
            ("keys", cache_keys, keys_v),
            ("values", cache_values, values_v),
            ("out", w_out, out_v),
            ("ffn", ffn_hbm, ffn_gain),
            ("gate", w_gate, gate_v),
            ("up", w_up, up_v),
            ("down", w_down, down_v),
        )
    ):
        pending[name] = pltpu.make_async_copy(source, target, load_sems.at[index])
        pending[name].start()

    def need(*names):
        for name in names:
            pending.pop(name).wait()

    sent = []

    def send_plane(phase, source, target):
        sent.append(phase)

        def one(index, carry):
            other_row, other_kv = plane_partner(index)
            pltpu.make_async_remote_copy(
                src_ref=source(other_row * kv_size + other_kv),
                dst_ref=target,
                send_sem=send_sems.at[phase],
                recv_sem=recv_sems.at[phase],
                device_id={"row": other_row, "kv": other_kv},
                device_id_type=MESH,
            ).start()
            return carry

        lax.fori_loop(0, plane - 1, one, 0)

    def send_tp(phase, source, target):
        sent.append(phase)

        def one(index, carry):
            pltpu.make_async_remote_copy(
                src_ref=source,
                dst_ref=target,
                send_sem=send_sems.at[phase],
                recv_sem=recv_sems.at[phase],
                device_id={"tp": lax.rem(tp + far_first(index, tp_size), tp_size)},
                device_id_type=MESH,
            ).start()
            return carry

        lax.fori_loop(0, tp_size - 1, one, 0)

    def whole(phase, part):
        return pltpu.make_async_remote_copy(
            src_ref=part,
            dst_ref=part,
            send_sem=send_sems.at[phase],
            recv_sem=recv_sems.at[phase],
            device_id={"tp": tp},
            device_id_type=MESH,
        )

    others = {
        0: r1.at[pl.ds(0, plane - 1)],
        1: r2.at[pl.ds(0, plane - 1)],
        2: r3.at[pl.ds(0, kv_size - 1)],
        3: r4.at[pl.ds(0, kv_size - 1)],
        4: r5.at[pl.ds(0, (plane - 1) * 8)],
        5: r6.at[pl.ds(0, tp_size - 1)],
        6: r7.at[pl.ds(0, plane - 1)],
        7: r8.at[pl.ds(0, plane - 1)],
        8: r9.at[pl.ds(0, tp_size - 1)],
    }

    def drain():
        for phase in sent:
            whole(phase, others[phase]).wait_send()

        if 1 in sent:
            @pl.when(owns_fresh)
            def _():
                whole(9, rf.at[pl.ds(0, 2 * row_size - 1)]).wait_send()

            @pl.when(jnp.logical_not(owns_fresh))
            def _():
                whole(9, rf.at[pl.ds(0, 2 * row_size)]).wait_send()

        if 2 in sent:
            @pl.when(owns_fresh)
            def _():
                whole(10, r3.at[pl.ds(0, kv_size - 1)]).wait_send()

    def arrived(phase):
        whole(phase, others[phase]).wait_recv()

    seqs = tokens.shape[0]
    width = tokens.shape[1]
    need("pool", "tokens")
    holder = jnp.zeros((seqs, seqs), jnp.int32)
    held = jnp.zeros((seqs, seqs), jnp.int32)
    for slot in range(seqs):
        seq = pool_smem[slot]
        holder = jnp.where(iota((seqs, seqs), 0) == slot, seq, holder)
        held = jnp.where(iota((seqs, seqs), 1) == slot, seq, held)
    to_slots = (holder == iota((seqs, seqs), 1)).astype(BF16)
    to_seqs = (held == iota((seqs, seqs), 0)).astype(BF16)
    stream = jnp.dot(to_slots, tokens[...], preferred_element_type=F32)

    wide = iota((seqs, HEAD), 0) == iota((seqs, HEAD), 1)

    def as_lanes(column):
        return jnp.sum(
            jnp.where(wide, jnp.broadcast_to(column, (seqs, HEAD)), 0.0), axis=0, keepdims=True
        )

    def as_column(lanes):
        return jnp.sum(
            jnp.where(wide, jnp.broadcast_to(lanes, (seqs, HEAD)), 0.0), axis=1, keepdims=True
        )

    squares = as_lanes(jnp.sum(stream * stream, axis=1, keepdims=True))
    s1[0] = squares
    r1[me] = squares

    pl.semaphore_wait(barrier, plane - 1 + tp_size - 1)

    send_plane(0, lambda other: s1.at[0], r1.at[me])
    arrived(0)
    first_sum = as_column(jnp.sum(r1[...], axis=0))
    need("attn", "len", "frequency", "qkv")
    gain = attn_gain[...].astype(F32).reshape(1, width)
    normed = (stream * lax.rsqrt(first_sum / D + EPSILON) * gain).astype(BF16)

    united = jnp.dot(normed, qkv_v[...], preferred_element_type=F32)
    for part in range(GROUP):
        s2[pl.ds(part, seqs, stride=GROUP), :] = united[:, part * HEAD : (part + 1) * HEAD]
    for part in range(2):
        sf[part] = united[:, (GROUP + part) * HEAD : (GROUP + part + 1) * HEAD]
    send_plane(1, lambda other: s2.at[pl.ds(pl.multiple_of(other * 8, 8), 8), :], r2.at[me])
    r2[me] = s2[pl.ds(pl.multiple_of(me * 8, 8), 8), :]

    def send_fresh(index, carry):
        owner_row, part = index // 2, lax.rem(index, 2)
        owner_kv = index

        @pl.when(jnp.logical_not((owner_row == row) & (owner_kv == kv)))
        def _():
            pltpu.make_async_remote_copy(
                src_ref=sf.at[part, pl.ds(pl.multiple_of(owner_row * kv_size, 8), kv_size), :],
                dst_ref=rf.at[me],
                send_sem=send_sems.at[9],
                recv_sem=recv_sems.at[9],
                device_id={"row": owner_row, "kv": owner_kv},
                device_id_type=MESH,
            ).start()

        return carry

    lax.fori_loop(0, 2 * row_size, send_fresh, 0)
    owns_fresh = kv // 2 == row
    fresh_part = lax.rem(kv, 2)
    lane_sign = jnp.where(iota((1, HEAD), 1) < HEAD // 2, -1.0, 1.0)
    angle = len_smem[pool_smem[me]].astype(F32) * frequency[...]
    cosine = jnp.cos(angle)
    sine = jnp.sin(angle) * lane_sign
    slots = kv_size
    limits = [len_smem[pool_smem[row * slots + slot]] for slot in range(slots)]
    arrived(1)
    mine = jnp.sum(r2[...], axis=0)
    mine = mine * cosine + pltpu.roll(mine, HEAD // 2, 1) * sine
    mine = jnp.concatenate([mine, jnp.zeros_like(mine)], axis=0).astype(BF16)

    s3[...] = mine
    r3[kv] = mine

    def query_copy(offset, target, index):
        return pltpu.make_async_remote_copy(
            src_ref=s3,
            dst_ref=r3.at[target],
            send_sem=send_sems.at[2],
            recv_sem=query_sems.at[index],
            device_id={"kv": lax.rem(kv + offset, kv_size)},
            device_id_type=MESH,
        )

    for index in range(kv_size - 1):
        offset = (4, 3, 5, 2, 6, 1, 7)[index]
        query_copy(offset, kv, kv_size - offset).start()
    sent.append(2)

    @pl.when(owns_fresh)
    def _():
        rf[me] = sf[fresh_part, pl.ds(pl.multiple_of(row * kv_size, 8), kv_size), :]
        column = jnp.zeros((slots, HEAD), jnp.int32)
        for slot in range(slots):
            column = jnp.where(iota((slots, HEAD), 0) == slot, limits[slot], column)
        angles = column.astype(F32) * frequency[...]
        cosines = jnp.where(fresh_part == 0, jnp.cos(angles), 1.0)
        sines = jnp.where(fresh_part == 0, jnp.sin(angles) * lane_sign, 0.0)
        whole(9, rf.at[pl.ds(0, plane - 1)]).wait_recv()
        fresh = jnp.sum(rf[...], axis=0)
        fresh = fresh * cosines + pltpu.roll(fresh, HEAD // 2, 1) * sines
        fresh = jnp.concatenate([fresh, jnp.zeros_like(fresh)], axis=0).astype(BF16)
        sp[...] = fresh
        rp[fresh_part] = fresh

        def share(step, carry):
            pltpu.make_async_remote_copy(
                src_ref=sp,
                dst_ref=rp.at[fresh_part],
                send_sem=send_sems.at[10],
                recv_sem=recv_sems.at[10],
                device_id={"kv": lax.rem(kv + step, kv_size)},
                device_id_type=MESH,
            ).start()
            return carry

        lax.fori_loop(1, kv_size, share, 0)

    need("keys", "values")
    block = keys_v.shape[1]
    score_scale = HEAD ** (-0.5)
    position = kv * block + iota((GROUP, block), 1)
    lane = iota((GROUP, HEAD), 1)
    for group in ((0,), (1, 7), (2, 6), (4,), (3, 5)):
        at = [lax.rem(kv + offset, kv_size) for offset in group]
        for offset, slot in zip(group, at):
            if offset:
                query_copy(offset, slot, offset).wait_recv()
        scores = [
            lax.dot_general(
                r3[slot, :GROUP, :],
                keys_v[slot],
                (((1,), (1,)), ((), ())),
                preferred_element_type=F32,
            )
            * score_scale
            for slot in at
        ]
        results = []
        for slot, score in zip(at, scores):
            limit = len_smem[pool_smem[row * slots + slot]]
            allowed = position < limit
            peak = jnp.max(jnp.where(allowed, score, FLOOR), axis=1, keepdims=True)
            weights = jnp.where(allowed, jnp.exp(score - peak), 0.0)
            total = jnp.sum(weights, axis=1, keepdims=True)
            product = jnp.dot(weights.astype(BF16), values_v[slot], preferred_element_type=F32)
            results.append((product, jnp.where(lane == 0, peak, total)))
        for offset, slot, (product, stats) in zip(group, at, results):
            if offset == 0:
                r4[kv, :GROUP] = product
                r4[kv, GROUP:] = stats
            else:
                s4[slot, :GROUP] = product
                s4[slot, GROUP:] = stats
                pltpu.make_async_remote_copy(
                    src_ref=s4.at[slot],
                    dst_ref=r4.at[kv],
                    send_sem=send_sems.at[3],
                    recv_sem=recv_sems.at[3],
                    device_id={"kv": slot},
                    device_id_type=MESH,
                ).start()
    sent.append(3)

    @pl.when(owns_fresh)
    def _():
        whole(10, rp.at[0]).wait_recv()

    @pl.when(jnp.logical_not(owns_fresh))
    def _():
        whole(10, rp).wait_recv()

    keys_out = pltpu.make_async_copy(rp.at[0], new_keys, out_sems.at[0])
    values_out = pltpu.make_async_copy(rp.at[1], new_values, out_sems.at[1])
    keys_out.start()
    values_out.start()
    this_slot = iota((slots, HEAD), 0) == kv
    fresh_key = jnp.sum(
        jnp.where(this_slot, rp[0].astype(F32)[:slots], 0.0), axis=0, keepdims=True
    )
    fresh_value = jnp.sum(
        jnp.where(this_slot, rp[1].astype(F32)[:slots], 0.0), axis=0, keepdims=True
    )
    fresh_query = mine.astype(F32)[:GROUP]
    fresh_score = jnp.sum(fresh_query * fresh_key, axis=1, keepdims=True) * score_scale
    arrived(3)
    parts = r4[...]
    peaks = [parts[source, GROUP:, 0:1] for source in range(slots)]
    joint = fresh_score
    for peak in peaks:
        joint = jnp.maximum(joint, peak)
    fresh_weight = jnp.exp(fresh_score - joint)
    total = fresh_weight
    numer = fresh_weight.astype(BF16).astype(F32) * fresh_value
    for source in range(slots):
        fade = jnp.exp(peaks[source] - joint)
        total = total + parts[source, GROUP:, 1:2] * fade
        numer = numer + parts[source, :GROUP] * fade
    mixed = numer / total

    s5[...] = mixed
    r5[pl.ds(pl.multiple_of(me * 8, 8), 8), :] = mixed
    send_plane(4, lambda other: s5, r5.at[pl.ds(pl.multiple_of(me * 8, 8), 8), :])
    need("out")
    arrived(4)
    mixed_all = jnp.concatenate(
        [r5[pl.ds(head, seqs, stride=8), :].astype(BF16) for head in range(GROUP)], axis=1
    )
    projected = jnp.dot(mixed_all, out_v[...], preferred_element_type=F32)

    projected = projected.astype(BF16)
    s6[...] = projected
    r6[tp] = projected
    send_tp(5, s6, r6.at[tp])
    need("ffn", "gate", "up")
    arrived(5)
    projected = r6[0].astype(F32)
    for source in range(1, tp_size):
        projected = projected + r6[source].astype(F32)
    stream_two = (stream + projected).astype(BF16).astype(F32)
    square_column = jnp.broadcast_to(
        jnp.sum(stream_two * stream_two, axis=1, keepdims=True), (seqs, HEAD)
    )
    scaled = (stream_two * ffn_gain[...].astype(F32).reshape(1, width)).astype(BF16)

    gate = jnp.dot(scaled, gate_v[...], preferred_element_type=F32)
    up = jnp.dot(scaled, up_v[...], preferred_element_type=F32)
    chunks = gate.shape[1] // HEAD
    for part in range(chunks):
        w7[pl.ds(part, seqs, stride=32), :] = gate[:, part * HEAD : (part + 1) * HEAD]
        w7[pl.ds(part + 16, seqs, stride=32), :] = up[:, part * HEAD : (part + 1) * HEAD]
    blank = jnp.zeros((seqs, HEAD), F32)
    high = square_column.astype(BF16).astype(F32)
    w7[pl.ds(14, seqs, stride=32), :] = high
    w7[pl.ds(15, seqs, stride=32), :] = square_column - high
    w7[pl.ds(30, seqs, stride=32), :] = blank
    w7[pl.ds(31, seqs, stride=32), :] = blank
    s7[...] = w7[...].astype(BF16)
    send_plane(6, lambda other: s7.at[pl.ds(pl.multiple_of(other * 32, 32), 32), :], r7.at[me])
    r7[me] = s7[pl.ds(pl.multiple_of(me * 32, 32), 32), :]
    need("down")
    arrived(6)
    sums = jnp.sum(r7[...].astype(F32), axis=0)
    scale = lax.rsqrt((sums[14:15] + sums[15:16]) / D + EPSILON)
    gate = sums[:16] * scale
    up = sums[16:] * scale
    activated = (gate / (1.0 + jnp.exp(-gate)) * up).astype(BF16)

    s8[...] = activated
    r8[me] = activated
    send_plane(7, lambda other: s8, r8.at[me])
    arrived(7)
    w8[...] = r8[...].astype(F32).reshape(w8.shape)
    active_all = jnp.concatenate(
        [w8[pl.ds(part, seqs, stride=16), :].astype(BF16) for part in range(chunks)], axis=1
    )
    down = jnp.dot(active_all, down_v[...], preferred_element_type=F32)

    down = down.astype(BF16)
    s9[...] = down
    r9[tp] = down
    send_tp(8, s9, r9.at[tp])
    arrived(8)
    down = r9[0].astype(F32)
    for source in range(1, tp_size):
        down = down + r9[source].astype(F32)
    result = (stream_two + down).astype(BF16)
    s_out[...] = jnp.dot(to_seqs, result, preferred_element_type=F32).astype(BF16)
    layer_copy = pltpu.make_async_copy(s_out, layer_out, out_sems.at[2])
    layer_copy.start()
    keys_out.wait()
    values_out.wait()
    layer_copy.wait()
    drain()


def local(
    sizes,
    tokens,
    attn_gain,
    w_qkv,
    w_out,
    ffn_gain,
    w_gate,
    w_up,
    w_down,
    cache_keys,
    cache_values,
    cache_len,
    pool_seq,
):
    tp_size, row_size, kv_size = sizes
    seqs, width = tokens.shape
    half = HEAD // 2
    pair = lax.rem(jnp.arange(HEAD, dtype=jnp.int32), half).astype(F32)
    frequency = (ROPE_BASE ** (-(pair * 2.0 / HEAD))).reshape(1, HEAD)
    plane = row_size * kv_size
    hbm = pl.BlockSpec(memory_space=pltpu.HBM)
    scratch = [
        pltpu.VMEM((1, HEAD), F32),
        pltpu.SMEM(pool_seq.shape, jnp.int32),
        pltpu.SMEM(cache_len.shape, jnp.int32),
        pltpu.VMEM(tokens.shape, BF16),
        pltpu.VMEM(attn_gain.shape, BF16),
        pltpu.VMEM(ffn_gain.shape, BF16),
        pltpu.VMEM(w_qkv.shape, BF16),
        pltpu.VMEM(w_out.shape, BF16),
        pltpu.VMEM(w_gate.shape, BF16),
        pltpu.VMEM(w_up.shape, BF16),
        pltpu.VMEM(w_down.shape, BF16),
        pltpu.VMEM(cache_keys.shape, BF16),
        pltpu.VMEM(cache_values.shape, BF16),
        pltpu.VMEM((1, 1, HEAD), F32),
        pltpu.VMEM((plane, 1, HEAD), F32),
        pltpu.VMEM((plane * 8, HEAD), F32),
        pltpu.VMEM((plane, 8, HEAD), F32),
        pltpu.VMEM((2, plane, HEAD), F32),
        pltpu.VMEM((plane, 8, HEAD), F32),
        pltpu.VMEM((16, HEAD), BF16),
        pltpu.VMEM((kv_size, 16, HEAD), BF16),
        pltpu.VMEM((16, HEAD), BF16),
        pltpu.VMEM((2, 16, HEAD), BF16),
        pltpu.VMEM((kv_size, 16, HEAD), F32),
        pltpu.VMEM((kv_size, 16, HEAD), F32),
        pltpu.VMEM((8, HEAD), F32),
        pltpu.VMEM((plane * 8, HEAD), F32),
        pltpu.VMEM((seqs, width), BF16),
        pltpu.VMEM((tp_size, seqs, width), BF16),
        pltpu.VMEM((plane * 32, HEAD), F32),
        pltpu.VMEM((plane * 32, HEAD), BF16),
        pltpu.VMEM((plane, 32, HEAD), BF16),
        pltpu.VMEM((16, HEAD), BF16),
        pltpu.VMEM((plane, 16, HEAD), BF16),
        pltpu.VMEM((plane * 16, HEAD), F32),
        pltpu.VMEM((seqs, width), BF16),
        pltpu.VMEM((tp_size, seqs, width), BF16),
        pltpu.VMEM((seqs, width), BF16),
        pltpu.SemaphoreType.DMA((13,)),
        pltpu.SemaphoreType.DMA((11,)),
        pltpu.SemaphoreType.DMA((11,)),
        pltpu.SemaphoreType.DMA((kv_size,)),
        pltpu.SemaphoreType.DMA((3,)),
    ]
    result, keys, values = pl.pallas_call(
        functools.partial(kernel, tp_size, row_size, kv_size),
        out_shape=(
            jax.ShapeDtypeStruct((seqs, width), BF16),
            jax.ShapeDtypeStruct((16, HEAD), BF16),
            jax.ShapeDtypeStruct((16, HEAD), BF16),
        ),
        in_specs=[hbm] * 13,
        out_specs=(hbm, hbm, hbm),
        scratch_shapes=scratch,
        compiler_params=pltpu.CompilerParams(
            collective_id=0, has_side_effects=True, vmem_limit_bytes=56 * 1024 * 1024
        ),
    )(
        frequency,
        pool_seq,
        cache_len,
        tokens,
        attn_gain,
        ffn_gain,
        w_qkv,
        w_out,
        w_gate,
        w_up,
        w_down,
        cache_keys,
        cache_values,
    )
    return result, keys[:kv_size], values[:kv_size]


def solution(mesh):
    sizes = (mesh.shape["tp"], mesh.shape["row"], mesh.shape["kv"])
    return jax.shard_map(
        functools.partial(local, sizes),
        mesh=mesh,
        in_specs=(
            P(None, ("row", "kv")),
            P(("row", "kv")),
            P(("row", "kv"), "tp"),
            P("tp", ("row", "kv")),
            P(("row", "kv")),
            P(("row", "kv"), "tp"),
            P(("row", "kv"), "tp"),
            P("tp", ("row", "kv")),
            P("row", "kv", "tp"),
            P("row", "kv", "tp"),
            P(),
            P(),
        ),
        out_specs=(P(None, ("row", "kv")), P("row", "tp"), P("row", "tp")),
        check_vma=False,
    )
```

```python
import functools

import jax
import jax.numpy as jnp
import numpy as np
from jax import lax
from jax.experimental import pallas as pl
from jax.experimental.pallas import tpu as pltpu
from jax.sharding import PartitionSpec as P

D = 8192
HEAD = 128
GROUP = 8
EPSILON = 1e-05
ROPE_BASE = 500000.0
FLOOR = -1e30
MESH = pl.DeviceIdType.MESH
F32 = jnp.float32
BF16 = jnp.bfloat16


def iota(shape, dim):
    return lax.broadcasted_iota(jnp.int32, shape, dim)


def far_first(index, size):
    half = (index + 1) // 2
    return size // 2 + (1 - 2 * lax.rem(index, 2)) * half


def kernel(
    tp_size,
    row_size,
    kv_size,
    frequency_hbm,
    pool_hbm,
    len_hbm,
    tokens_hbm,
    attn_hbm,
    ffn_hbm,
    w_qkv,
    w_out,
    w_gate,
    w_up,
    w_down,
    cache_keys,
    cache_values,
    layer_out,
    new_keys,
    new_values,
    frequency,
    pool_smem,
    len_smem,
    tokens,
    attn_gain,
    ffn_gain,
    qkv_v,
    out_v,
    gate_v,
    up_v,
    down_v,
    keys_v,
    values_v,
    s1,
    r1,
    s2,
    r2,
    sf,
    rf,
    s3,
    r3,
    sp,
    rp,
    s4,
    r4,
    s5,
    r5,
    s6,
    r6,
    w7,
    s7,
    r7,
    s8,
    r8,
    w8,
    s9,
    r9,
    load_sems,
    send_sems,
    recv_sems,
    query_sems,
):
    plane = row_size * kv_size
    tp = lax.axis_index("tp")
    row = lax.axis_index("row")
    kv = lax.axis_index("kv")
    me = row * kv_size + kv

    barrier = pltpu.get_barrier_semaphore()

    def plane_partner(index):
        other_row = lax.rem(row + far_first(lax.rem(index, row_size), row_size), row_size)
        other_kv = lax.rem(kv + far_first(index // row_size, kv_size), kv_size)
        return other_row, other_kv

    def greet_plane(index, carry):
        other_row, other_kv = plane_partner(index)
        pl.semaphore_signal(
            barrier,
            inc=1,
            device_id={"row": other_row, "kv": other_kv},
            device_id_type=MESH,
        )
        return carry

    def greet_tp(step, carry):
        pl.semaphore_signal(
            barrier, inc=1, device_id={"tp": lax.rem(tp + step, tp_size)}, device_id_type=MESH
        )
        return carry

    lax.fori_loop(0, plane - 1, greet_plane, 0)
    lax.fori_loop(1, tp_size, greet_tp, 0)

    pending = {}
    for index, (name, source, target) in enumerate(
        (
            ("pool", pool_hbm, pool_smem),
            ("tokens", tokens_hbm, tokens),
            ("len", len_hbm, len_smem),
            ("attn", attn_hbm, attn_gain),
            ("frequency", frequency_hbm, frequency),
            ("qkv", w_qkv, qkv_v),
            ("keys", cache_keys, keys_v),
            ("values", cache_values, values_v),
            ("out", w_out, out_v),
            ("ffn", ffn_hbm, ffn_gain),
            ("gate", w_gate, gate_v),
            ("up", w_up, up_v),
            ("down", w_down, down_v),
        )
    ):
        pending[name] = pltpu.make_async_copy(source, target, load_sems.at[index])
        pending[name].start()

    def need(*names):
        for name in names:
            pending.pop(name).wait()

    sent = []

    def send_plane(phase, source, target):
        sent.append(phase)

        def one(index, carry):
            other_row, other_kv = plane_partner(index)
            pltpu.make_async_remote_copy(
                src_ref=source(other_row * kv_size + other_kv),
                dst_ref=target,
                send_sem=send_sems.at[phase],
                recv_sem=recv_sems.at[phase],
                device_id={"row": other_row, "kv": other_kv},
                device_id_type=MESH,
            ).start()
            return carry

        lax.fori_loop(0, plane - 1, one, 0)

    def send_tp(phase, source, target):
        sent.append(phase)

        def one(index, carry):
            pltpu.make_async_remote_copy(
                src_ref=source,
                dst_ref=target,
                send_sem=send_sems.at[phase],
                recv_sem=recv_sems.at[phase],
                device_id={"tp": lax.rem(tp + far_first(index, tp_size), tp_size)},
                device_id_type=MESH,
            ).start()
            return carry

        lax.fori_loop(0, tp_size - 1, one, 0)

    def whole(phase, part):
        return pltpu.make_async_remote_copy(
            src_ref=part,
            dst_ref=part,
            send_sem=send_sems.at[phase],
            recv_sem=recv_sems.at[phase],
            device_id={"tp": tp},
            device_id_type=MESH,
        )

    others = {
        0: r1.at[pl.ds(0, plane - 1)],
        1: r2.at[pl.ds(0, plane - 1)],
        2: r3.at[pl.ds(0, kv_size - 1)],
        3: r4.at[pl.ds(0, kv_size - 1)],
        4: r5.at[pl.ds(0, (plane - 1) * 8)],
        5: r6.at[0, pl.ds(0, tp_size - 1)],
        11: r6.at[1, pl.ds(0, tp_size - 1)],
        6: r7.at[pl.ds(0, plane - 1)],
        7: r8.at[pl.ds(0, plane - 1)],
        8: r9.at[0, pl.ds(0, tp_size - 1)],
        12: r9.at[1, pl.ds(0, tp_size - 1)],
    }

    def drain():
        for phase in sent:
            whole(phase, others[phase]).wait_send()

        if 1 in sent:
            @pl.when(owns_fresh)
            def _():
                whole(9, rf.at[pl.ds(0, 2 * row_size - 1)]).wait_send()

            @pl.when(jnp.logical_not(owns_fresh))
            def _():
                whole(9, rf.at[pl.ds(0, 2 * row_size)]).wait_send()

        if 2 in sent:
            @pl.when(owns_fresh)
            def _():
                whole(10, r3.at[pl.ds(0, kv_size - 1)]).wait_send()

    def arrived(phase):
        whole(phase, others[phase]).wait_recv()

    seqs = tokens.shape[0]
    width = tokens.shape[1]
    need("pool", "tokens")
    holder = jnp.zeros((seqs, seqs), jnp.int32)
    held = jnp.zeros((seqs, seqs), jnp.int32)
    for slot in range(seqs):
        seq = pool_smem[slot]
        holder = jnp.where(iota((seqs, seqs), 0) == slot, seq, holder)
        held = jnp.where(iota((seqs, seqs), 1) == slot, seq, held)
    to_slots = (holder == iota((seqs, seqs), 1)).astype(BF16)
    to_seqs = (held == iota((seqs, seqs), 0)).astype(BF16)
    stream = jnp.dot(to_slots, tokens[...], preferred_element_type=F32)

    wide = iota((seqs, HEAD), 0) == iota((seqs, HEAD), 1)

    def as_lanes(column):
        return jnp.sum(
            jnp.where(wide, jnp.broadcast_to(column, (seqs, HEAD)), 0.0), axis=0, keepdims=True
        )

    def as_column(lanes):
        return jnp.sum(
            jnp.where(wide, jnp.broadcast_to(lanes, (seqs, HEAD)), 0.0), axis=1, keepdims=True
        )

    squares = as_lanes(jnp.sum(stream * stream, axis=1, keepdims=True))
    s1[0] = squares
    r1[me] = squares

    pl.semaphore_wait(barrier, plane - 1 + tp_size - 1)

    send_plane(0, lambda other: s1.at[0], r1.at[me])
    arrived(0)
    first_sum = as_column(jnp.sum(r1[...], axis=0))
    need("attn", "len", "frequency", "qkv")
    gain = attn_gain[...].astype(F32).reshape(1, width)
    normed = (stream * lax.rsqrt(first_sum / D + EPSILON) * gain).astype(BF16)

    united = jnp.dot(normed, qkv_v[...], preferred_element_type=F32)
    for part in range(GROUP):
        s2[pl.ds(part, seqs, stride=GROUP), :] = united[:, part * HEAD : (part + 1) * HEAD]
    for part in range(2):
        sf[part] = united[:, (GROUP + part) * HEAD : (GROUP + part + 1) * HEAD]
    send_plane(1, lambda other: s2.at[pl.ds(pl.multiple_of(other * 8, 8), 8), :], r2.at[me])
    r2[me] = s2[pl.ds(pl.multiple_of(me * 8, 8), 8), :]

    def send_fresh(index, carry):
        owner_row, part = index // 2, lax.rem(index, 2)
        owner_kv = index

        @pl.when(jnp.logical_not((owner_row == row) & (owner_kv == kv)))
        def _():
            pltpu.make_async_remote_copy(
                src_ref=sf.at[part, pl.ds(pl.multiple_of(owner_row * kv_size, 8), kv_size), :],
                dst_ref=rf.at[me],
                send_sem=send_sems.at[9],
                recv_sem=recv_sems.at[9],
                device_id={"row": owner_row, "kv": owner_kv},
                device_id_type=MESH,
            ).start()

        return carry

    lax.fori_loop(0, 2 * row_size, send_fresh, 0)
    owns_fresh = kv // 2 == row
    fresh_part = lax.rem(kv, 2)
    lane_sign = jnp.where(iota((1, HEAD), 1) < HEAD // 2, -1.0, 1.0)
    angle = len_smem[pool_smem[me]].astype(F32) * frequency[...]
    cosine = jnp.cos(angle)
    sine = jnp.sin(angle) * lane_sign
    slots = kv_size
    limits = [len_smem[pool_smem[row * slots + slot]] for slot in range(slots)]
    arrived(1)
    mine = jnp.sum(r2[...], axis=0)
    mine = mine * cosine + pltpu.roll(mine, HEAD // 2, 1) * sine
    mine = jnp.concatenate([mine, jnp.zeros_like(mine)], axis=0).astype(BF16)

    s3[...] = mine
    r3[kv] = mine

    def query_copy(offset, target, index):
        return pltpu.make_async_remote_copy(
            src_ref=s3,
            dst_ref=r3.at[target],
            send_sem=send_sems.at[2],
            recv_sem=query_sems.at[index],
            device_id={"kv": lax.rem(kv + offset, kv_size)},
            device_id_type=MESH,
        )

    for index in range(kv_size - 1):
        offset = (4, 3, 5, 2, 6, 1, 7)[index]
        query_copy(offset, kv, kv_size - offset).start()
    sent.append(2)

    @pl.when(owns_fresh)
    def _():
        rf[me] = sf[fresh_part, pl.ds(pl.multiple_of(row * kv_size, 8), kv_size), :]
        column = jnp.zeros((slots, HEAD), jnp.int32)
        for slot in range(slots):
            column = jnp.where(iota((slots, HEAD), 0) == slot, limits[slot], column)
        angles = column.astype(F32) * frequency[...]
        cosines = jnp.where(fresh_part == 0, jnp.cos(angles), 1.0)
        sines = jnp.where(fresh_part == 0, jnp.sin(angles) * lane_sign, 0.0)
        whole(9, rf.at[pl.ds(0, plane - 1)]).wait_recv()
        fresh = jnp.sum(rf[...], axis=0)
        fresh = fresh * cosines + pltpu.roll(fresh, HEAD // 2, 1) * sines
        fresh = jnp.concatenate([fresh, jnp.zeros_like(fresh)], axis=0).astype(BF16)
        sp[...] = fresh
        rp[fresh_part] = fresh

        def share(step, carry):
            pltpu.make_async_remote_copy(
                src_ref=sp,
                dst_ref=rp.at[fresh_part],
                send_sem=send_sems.at[10],
                recv_sem=recv_sems.at[10],
                device_id={"kv": lax.rem(kv + step, kv_size)},
                device_id_type=MESH,
            ).start()
            return carry

        lax.fori_loop(1, kv_size, share, 0)

    need("keys", "values")
    block = keys_v.shape[1]
    score_scale = HEAD ** (-0.5)
    position = kv * block + iota((GROUP, block), 1)
    lane = iota((GROUP, HEAD), 1)
    for group in ((0,), (1, 7), (2, 6), (4,), (3, 5)):
        at = [lax.rem(kv + offset, kv_size) for offset in group]
        for offset, slot in zip(group, at):
            if offset:
                query_copy(offset, slot, offset).wait_recv()
        scores = [
            lax.dot_general(
                r3[slot, :GROUP, :],
                keys_v[slot],
                (((1,), (1,)), ((), ())),
                preferred_element_type=F32,
            )
            * score_scale
            for slot in at
        ]
        results = []
        for slot, score in zip(at, scores):
            limit = len_smem[pool_smem[row * slots + slot]]
            allowed = position < limit
            peak = jnp.max(jnp.where(allowed, score, FLOOR), axis=1, keepdims=True)
            weights = jnp.where(allowed, jnp.exp(score - peak), 0.0)
            total = jnp.sum(weights, axis=1, keepdims=True)
            product = jnp.dot(weights.astype(BF16), values_v[slot], preferred_element_type=F32)
            results.append((product, jnp.where(lane == 0, peak, total)))
        for offset, slot, (product, stats) in zip(group, at, results):
            if offset == 0:
                r4[kv, :GROUP] = product
                r4[kv, GROUP:] = stats
            else:
                s4[slot, :GROUP] = product
                s4[slot, GROUP:] = stats
                pltpu.make_async_remote_copy(
                    src_ref=s4.at[slot],
                    dst_ref=r4.at[kv],
                    send_sem=send_sems.at[3],
                    recv_sem=recv_sems.at[3],
                    device_id={"kv": slot},
                    device_id_type=MESH,
                ).start()
    sent.append(3)

    @pl.when(owns_fresh)
    def _():
        whole(10, rp.at[0]).wait_recv()

    @pl.when(jnp.logical_not(owns_fresh))
    def _():
        whole(10, rp).wait_recv()

    new_keys[...] = rp[0][:slots]
    new_values[...] = rp[1][:slots]
    this_slot = iota((slots, HEAD), 0) == kv
    fresh_key = jnp.sum(
        jnp.where(this_slot, rp[0].astype(F32)[:slots], 0.0), axis=0, keepdims=True
    )
    fresh_value = jnp.sum(
        jnp.where(this_slot, rp[1].astype(F32)[:slots], 0.0), axis=0, keepdims=True
    )
    fresh_query = mine.astype(F32)[:GROUP]
    fresh_score = jnp.sum(fresh_query * fresh_key, axis=1, keepdims=True) * score_scale
    arrived(3)
    parts = r4[...]
    peaks = [parts[source, GROUP:, 0:1] for source in range(slots)]
    joint = fresh_score
    for peak in peaks:
        joint = jnp.maximum(joint, peak)
    fresh_weight = jnp.exp(fresh_score - joint)
    total = fresh_weight
    numer = fresh_weight.astype(BF16).astype(F32) * fresh_value
    for source in range(slots):
        fade = jnp.exp(peaks[source] - joint)
        total = total + parts[source, GROUP:, 1:2] * fade
        numer = numer + parts[source, :GROUP] * fade
    mixed = numer / total

    s5[...] = mixed
    r5[pl.ds(pl.multiple_of(me * 8, 8), 8), :] = mixed
    send_plane(4, lambda other: s5, r5.at[pl.ds(pl.multiple_of(me * 8, 8), 8), :])
    need("out")
    arrived(4)
    mixed_all = jnp.concatenate(
        [r5[pl.ds(head, seqs, stride=8), :].astype(BF16) for head in range(GROUP)], axis=1
    )
    projected = jnp.dot(mixed_all, out_v[...], preferred_element_type=F32)

    half = seqs // 2
    half_rows = row_size // 2
    my_block = row // half_rows

    projected = projected.astype(BF16)
    for block, phase in enumerate((5, 11)):
        part = projected[block * half : (block + 1) * half]
        s6[block] = part
        r6[block, tp] = part
        send_tp(phase, s6.at[block], r6.at[block, tp])
    need("ffn", "gate", "up")
    ffn = ffn_gain[...].astype(F32).reshape(1, width)
    blank = jnp.zeros((half, HEAD), F32)
    chunks = gate_v.shape[1] // HEAD
    streams = []
    for block, phase in enumerate((5, 11)):
        arrived(phase)
        total = r6[block, 0].astype(F32)
        for source in range(1, tp_size):
            total = total + r6[block, source].astype(F32)
        rows = (stream[block * half : (block + 1) * half] + total).astype(BF16).astype(F32)
        streams.append(rows)
        square_column = jnp.broadcast_to(
            jnp.sum(rows * rows, axis=1, keepdims=True), (half, HEAD)
        )
        scaled = (rows * ffn).astype(BF16)

        gate = jnp.dot(scaled, gate_v[...], preferred_element_type=F32)
        up = jnp.dot(scaled, up_v[...], preferred_element_type=F32)
        base = block * half * 32
        for part in range(chunks):
            columns = slice(part * HEAD, (part + 1) * HEAD)
            w7[pl.ds(base + part, half, stride=32), :] = gate[:, columns]
            w7[pl.ds(base + part + 16, half, stride=32), :] = up[:, columns]
        high = square_column.astype(BF16).astype(F32)
        w7[pl.ds(base + 14, half, stride=32), :] = high
        w7[pl.ds(base + 15, half, stride=32), :] = square_column - high
        w7[pl.ds(base + 30, half, stride=32), :] = blank
        w7[pl.ds(base + 31, half, stride=32), :] = blank
        s7[base : base + half * 32, :] = w7[base : base + half * 32, :].astype(BF16)

        def send_partial(index, carry, block=block):
            other_row = block * half_rows + lax.rem(index, half_rows)
            other_kv = lax.rem(kv + far_first(index // half_rows, kv_size), kv_size)
            other = other_row * kv_size + other_kv

            @pl.when(other != me)
            def _():
                pltpu.make_async_remote_copy(
                    src_ref=s7.at[pl.ds(pl.multiple_of(other * 32, 32), 32), :],
                    dst_ref=r7.at[me],
                    send_sem=send_sems.at[6],
                    recv_sem=recv_sems.at[6],
                    device_id={"row": other_row, "kv": other_kv},
                    device_id_type=MESH,
                ).start()

            return carry

        lax.fori_loop(0, half, send_partial, 0)
    sent.append(6)
    r7[me] = s7[pl.ds(pl.multiple_of(me * 32, 32), 32), :]
    need("down")
    arrived(6)
    sums = jnp.sum(r7[...].astype(F32), axis=0)
    scale = lax.rsqrt((sums[14:15] + sums[15:16]) / D + EPSILON)
    gate = sums[:16] * scale
    up = sums[16:] * scale
    activated = (gate / (1.0 + jnp.exp(-gate)) * up).astype(BF16)

    s8[...] = activated
    r8[me] = activated
    def share_activated(index, carry):
        other_row, other_kv = plane_partner(index)
        pltpu.make_async_remote_copy(
            src_ref=s8,
            dst_ref=r8.at[me],
            send_sem=send_sems.at[7],
            recv_sem=recv_sems.at[7 + 6 * my_block],
            device_id={"row": other_row, "kv": other_kv},
            device_id_type=MESH,
        ).start()
        return carry

    lax.fori_loop(0, plane - 1, share_activated, 0)
    sent.append(7)
    for block, phase in enumerate((8, 12)):

        @pl.when(my_block == block)
        def _(block=block):
            whole(7 + 6 * block, r8.at[pl.ds(0, half - 1)]).wait_recv()

        @pl.when(my_block != block)
        def _(block=block):
            whole(7 + 6 * block, r8.at[pl.ds(0, half)]).wait_recv()

        w8[...] = r8[block * half : (block + 1) * half].astype(F32).reshape(w8.shape)
        active = jnp.concatenate(
            [w8[pl.ds(part, half, stride=16), :].astype(BF16) for part in range(chunks)], axis=1
        )
        down = jnp.dot(active, down_v[...], preferred_element_type=F32).astype(BF16)

        s9[block] = down
        r9[block, tp] = down
        send_tp(phase, s9.at[block], r9.at[block, tp])
    results = []
    for block, phase in enumerate((8, 12)):
        arrived(phase)
        total = r9[block, 0].astype(F32)
        for source in range(1, tp_size):
            total = total + r9[block, source].astype(F32)
        results.append((streams[block] + total).astype(BF16))
    result = jnp.concatenate(results, axis=0)
    layer_out[...] = jnp.dot(to_seqs, result, preferred_element_type=F32).astype(BF16)
    drain()


def hand_out(result, keys, values, layer_out, new_keys, new_values, sems):
    copies = [
        pltpu.make_async_copy(result, layer_out, sems.at[0]),
        pltpu.make_async_copy(keys, new_keys, sems.at[1]),
        pltpu.make_async_copy(values, new_values, sems.at[2]),
    ]
    for copy in copies:
        copy.start()
    for copy in copies:
        copy.wait()


def local(
    sizes,
    tokens,
    attn_gain,
    w_qkv,
    w_out,
    ffn_gain,
    w_gate,
    w_up,
    w_down,
    cache_keys,
    cache_values,
    cache_len,
    pool_seq,
):
    tp_size, row_size, kv_size = sizes
    seqs, width = tokens.shape
    pair = np.arange(HEAD) % (HEAD // 2)
    frequency = (ROPE_BASE ** (-2.0 * pair / HEAD)).astype(np.float32).reshape(1, HEAD)
    plane = row_size * kv_size
    vmem = pl.BlockSpec(memory_space=pltpu.VMEM)
    hbm = pl.BlockSpec(memory_space=pltpu.HBM)
    scratch = [
        pltpu.VMEM((1, HEAD), F32),
        pltpu.SMEM(pool_seq.shape, jnp.int32),
        pltpu.SMEM(cache_len.shape, jnp.int32),
        pltpu.VMEM(tokens.shape, BF16),
        pltpu.VMEM(attn_gain.shape, BF16),
        pltpu.VMEM(ffn_gain.shape, BF16),
        pltpu.VMEM(w_qkv.shape, BF16),
        pltpu.VMEM(w_out.shape, BF16),
        pltpu.VMEM(w_gate.shape, BF16),
        pltpu.VMEM(w_up.shape, BF16),
        pltpu.VMEM(w_down.shape, BF16),
        pltpu.VMEM(cache_keys.shape, BF16),
        pltpu.VMEM(cache_values.shape, BF16),
        pltpu.VMEM((1, 1, HEAD), F32),
        pltpu.VMEM((plane, 1, HEAD), F32),
        pltpu.VMEM((plane * 8, HEAD), F32),
        pltpu.VMEM((plane, 8, HEAD), F32),
        pltpu.VMEM((2, plane, HEAD), F32),
        pltpu.VMEM((plane, 8, HEAD), F32),
        pltpu.VMEM((16, HEAD), BF16),
        pltpu.VMEM((kv_size, 16, HEAD), BF16),
        pltpu.VMEM((16, HEAD), BF16),
        pltpu.VMEM((2, 16, HEAD), BF16),
        pltpu.VMEM((kv_size, 16, HEAD), F32),
        pltpu.VMEM((kv_size, 16, HEAD), F32),
        pltpu.VMEM((8, HEAD), F32),
        pltpu.VMEM((plane * 8, HEAD), F32),
        pltpu.VMEM((2, seqs // 2, width), BF16),
        pltpu.VMEM((2, tp_size, seqs // 2, width), BF16),
        pltpu.VMEM((plane * 32, HEAD), F32),
        pltpu.VMEM((plane * 32, HEAD), BF16),
        pltpu.VMEM((plane, 32, HEAD), BF16),
        pltpu.VMEM((16, HEAD), BF16),
        pltpu.VMEM((plane, 16, HEAD), BF16),
        pltpu.VMEM((plane * 8, HEAD), F32),
        pltpu.VMEM((2, seqs // 2, width), BF16),
        pltpu.VMEM((2, tp_size, seqs // 2, width), BF16),
        pltpu.SemaphoreType.DMA((13,)),
        pltpu.SemaphoreType.DMA((14,)),
        pltpu.SemaphoreType.DMA((14,)),
        pltpu.SemaphoreType.DMA((kv_size,)),
    ]
    result, keys, values = pl.pallas_call(
        functools.partial(kernel, tp_size, row_size, kv_size),
        out_shape=(
            jax.ShapeDtypeStruct((seqs, width), BF16),
            jax.ShapeDtypeStruct((kv_size, HEAD), BF16),
            jax.ShapeDtypeStruct((kv_size, HEAD), BF16),
        ),
        in_specs=[hbm] * 13,
        out_specs=(vmem, vmem, vmem),
        scratch_shapes=scratch,
        compiler_params=pltpu.CompilerParams(
            collective_id=0, has_side_effects=True, vmem_limit_bytes=24 * 1024 * 1024
        ),
    )(
        *(
            pltpu.with_memory_space_constraint(part, pltpu.HBM)
            for part in (
                frequency,
                pool_seq,
                cache_len,
                tokens,
                attn_gain,
                ffn_gain,
                w_qkv,
                w_out,
                w_gate,
                w_up,
                w_down,
                cache_keys,
                cache_values,
            )
        )
    )
    return pl.pallas_call(
        hand_out,
        out_shape=(
            jax.ShapeDtypeStruct((seqs, width), BF16),
            jax.ShapeDtypeStruct((kv_size, HEAD), BF16),
            jax.ShapeDtypeStruct((kv_size, HEAD), BF16),
        ),
        in_specs=[vmem] * 3,
        out_specs=(hbm, hbm, hbm),
        scratch_shapes=[pltpu.SemaphoreType.DMA((3,))],
    )(*(pltpu.with_memory_space_constraint(part, pltpu.VMEM) for part in (result, keys, values)))


def solution(mesh):
    sizes = (mesh.shape["tp"], mesh.shape["row"], mesh.shape["kv"])
    return jax.shard_map(
        functools.partial(local, sizes),
        mesh=mesh,
        in_specs=(
            P(None, ("row", "kv")),
            P(("row", "kv")),
            P(("row", "kv"), "tp"),
            P("tp", ("row", "kv")),
            P(("row", "kv")),
            P(("row", "kv"), "tp"),
            P(("row", "kv"), "tp"),
            P("tp", ("row", "kv")),
            P("row", "kv", "tp"),
            P("row", "kv", "tp"),
            P(),
            P(),
        ),
        out_specs=(P(None, ("row", "kv")), P("row", "tp"), P("row", "tp")),
        check_vma=False,
    )
```

```python
import functools

import jax
import jax.numpy as jnp
import numpy as np
from jax import lax
from jax.experimental import pallas as pl
from jax.experimental.pallas import tpu as pltpu
from jax.sharding import PartitionSpec as P

D = 8192
HEAD = 128
GROUP = 8
EPSILON = 1e-05
ROPE_BASE = 500000.0
FLOOR = -1e30
MESH = pl.DeviceIdType.MESH
F32 = jnp.float32
BF16 = jnp.bfloat16


def iota(shape, dim):
    return lax.broadcasted_iota(jnp.int32, shape, dim)


def far_first(index, size):
    half = (index + 1) // 2
    return size // 2 + (1 - 2 * lax.rem(index, 2)) * half


def kernel(
    tp_size,
    row_size,
    kv_size,
    frequency_hbm,
    pool_hbm,
    len_hbm,
    tokens_hbm,
    attn_hbm,
    ffn_hbm,
    w_qkv,
    w_out,
    w_gate,
    w_up,
    w_down,
    cache_keys,
    cache_values,
    layer_out,
    new_keys,
    new_values,
    frequency,
    pool_smem,
    len_smem,
    tokens,
    attn_gain,
    ffn_gain,
    qkv_v,
    out_v,
    gate_v,
    up_v,
    down_v,
    keys_v,
    values_v,
    s1,
    r1,
    s2,
    r2,
    sf,
    rf,
    s3,
    r3,
    sp,
    rp,
    s4,
    r4,
    s5,
    r5,
    s6,
    r6,
    w7,
    s7,
    r7,
    s8,
    r8,
    w8,
    s9,
    r9,
    load_sems,
    send_sems,
    recv_sems,
    query_sems,
):
    plane = row_size * kv_size
    tp = lax.axis_index("tp")
    row = lax.axis_index("row")
    kv = lax.axis_index("kv")
    me = row * kv_size + kv

    barrier = pltpu.get_barrier_semaphore()

    def plane_partner(index):
        other_row = lax.rem(row + far_first(lax.rem(index, row_size), row_size), row_size)
        other_kv = lax.rem(kv + far_first(index // row_size, kv_size), kv_size)
        return other_row, other_kv

    def greet_plane(index, carry):
        other_row, other_kv = plane_partner(index)
        pl.semaphore_signal(
            barrier,
            inc=1,
            device_id={"row": other_row, "kv": other_kv},
            device_id_type=MESH,
        )
        return carry

    def greet_tp(step, carry):
        pl.semaphore_signal(
            barrier, inc=1, device_id={"tp": lax.rem(tp + step, tp_size)}, device_id_type=MESH
        )
        return carry

    lax.fori_loop(0, plane - 1, greet_plane, 0)
    lax.fori_loop(1, tp_size, greet_tp, 0)

    pending = {}
    for index, (name, source, target) in enumerate(
        (
            ("pool", pool_hbm, pool_smem),
            ("tokens", tokens_hbm, tokens),
            ("len", len_hbm, len_smem),
            ("attn", attn_hbm, attn_gain),
            ("frequency", frequency_hbm, frequency),
            ("qkv", w_qkv, qkv_v),
            ("keys", cache_keys, keys_v),
            ("values", cache_values, values_v),
            ("out", w_out, out_v),
            ("ffn", ffn_hbm, ffn_gain),
            ("gate", w_gate, gate_v),
            ("up", w_up, up_v),
            ("down", w_down, down_v),
        )
    ):
        pending[name] = pltpu.make_async_copy(source, target, load_sems.at[index])
        pending[name].start()

    def need(*names):
        for name in names:
            pending.pop(name).wait()

    sent = []

    def send_plane(phase, source, target):
        sent.append(phase)

        def one(index, carry):
            other_row, other_kv = plane_partner(index)
            pltpu.make_async_remote_copy(
                src_ref=source(other_row * kv_size + other_kv),
                dst_ref=target,
                send_sem=send_sems.at[phase],
                recv_sem=recv_sems.at[phase],
                device_id={"row": other_row, "kv": other_kv},
                device_id_type=MESH,
            ).start()
            return carry

        lax.fori_loop(0, plane - 1, one, 0)

    def send_tp(phase, source, target):
        sent.append(phase)

        def one(index, carry):
            pltpu.make_async_remote_copy(
                src_ref=source,
                dst_ref=target,
                send_sem=send_sems.at[phase],
                recv_sem=recv_sems.at[phase],
                device_id={"tp": lax.rem(tp + far_first(index, tp_size), tp_size)},
                device_id_type=MESH,
            ).start()
            return carry

        lax.fori_loop(0, tp_size - 1, one, 0)

    def whole(phase, part):
        return pltpu.make_async_remote_copy(
            src_ref=part,
            dst_ref=part,
            send_sem=send_sems.at[phase],
            recv_sem=recv_sems.at[phase],
            device_id={"tp": tp},
            device_id_type=MESH,
        )

    others = {
        0: r1.at[pl.ds(0, plane - 1)],
        1: r2.at[pl.ds(0, plane - 1)],
        2: r3.at[pl.ds(0, kv_size - 1)],
        3: r4.at[pl.ds(0, 2 * (kv_size - 1))],
        4: r5.at[pl.ds(0, plane // 2 - 1)],
        5: r6.at[0, pl.ds(0, tp_size - 1)],
        11: r6.at[1, pl.ds(0, tp_size - 1)],
        6: r7.at[pl.ds(0, plane - 1)],
        7: r8.at[pl.ds(0, plane - 1)],
        8: r9.at[0, pl.ds(0, tp_size - 1)],
        12: r9.at[1, pl.ds(0, tp_size - 1)],
    }

    def drain():
        for phase in sent:
            whole(phase, others[phase]).wait_send()

        if 1 in sent:
            @pl.when(owns_fresh)
            def _():
                whole(9, rf.at[pl.ds(0, 2 * row_size - 1)]).wait_send()

            @pl.when(jnp.logical_not(owns_fresh))
            def _():
                whole(9, rf.at[pl.ds(0, 2 * row_size)]).wait_send()

        if 2 in sent:
            @pl.when(owns_fresh)
            def _():
                whole(10, r3.at[pl.ds(0, kv_size - 1)]).wait_send()

    def arrived(phase):
        whole(phase, others[phase]).wait_recv()

    seqs = tokens.shape[0]
    width = tokens.shape[1]
    need("pool", "tokens")
    holder = jnp.zeros((seqs, seqs), jnp.int32)
    for slot in range(seqs):
        holder = jnp.where(iota((seqs, seqs), 0) == slot, pool_smem[slot], holder)
    to_slots = (holder == iota((seqs, seqs), 1)).astype(BF16)
    stream = jnp.dot(to_slots, tokens[...], preferred_element_type=F32)
    quarter = kv_size // 2
    holder = jnp.zeros((seqs, seqs), jnp.int32)
    held = jnp.zeros((seqs, seqs), jnp.int32)
    for index in range(seqs):
        group, place = index // kv_size, index % kv_size
        seq = pool_smem[group * kv_size + place // 2 + quarter * (place % 2)]
        holder = jnp.where(iota((seqs, seqs), 0) == index, seq, holder)
        held = jnp.where(iota((seqs, seqs), 1) == index, seq, held)
    to_pairs = (holder == iota((seqs, seqs), 1)).astype(BF16)
    to_seqs = (held == iota((seqs, seqs), 0)).astype(BF16)
    stream_pairs = jnp.dot(to_pairs, tokens[...], preferred_element_type=F32)

    wide = iota((seqs, HEAD), 0) == iota((seqs, HEAD), 1)

    def as_lanes(column):
        return jnp.sum(
            jnp.where(wide, jnp.broadcast_to(column, (seqs, HEAD)), 0.0), axis=0, keepdims=True
        )

    def as_column(lanes):
        return jnp.sum(
            jnp.where(wide, jnp.broadcast_to(lanes, (seqs, HEAD)), 0.0), axis=1, keepdims=True
        )

    squares = as_lanes(jnp.sum(stream * stream, axis=1, keepdims=True))
    s1[0] = squares
    r1[me] = squares

    pl.semaphore_wait(barrier, plane - 1 + tp_size - 1)

    send_plane(0, lambda other: s1.at[0], r1.at[me])
    arrived(0)
    first_sum = as_column(jnp.sum(r1[...], axis=0))
    need("attn", "len", "frequency", "qkv")
    gain = attn_gain[...].astype(F32).reshape(1, width)
    normed = (stream * lax.rsqrt(first_sum / D + EPSILON) * gain).astype(BF16)

    united = jnp.dot(normed, qkv_v[...], preferred_element_type=F32)
    for part in range(GROUP):
        s2[pl.ds(part, seqs, stride=GROUP), :] = united[:, part * HEAD : (part + 1) * HEAD]
    for part in range(2):
        sf[part] = united[:, (GROUP + part) * HEAD : (GROUP + part + 1) * HEAD]
    send_plane(1, lambda other: s2.at[pl.ds(pl.multiple_of(other * 8, 8), 8), :], r2.at[me])
    r2[me] = s2[pl.ds(pl.multiple_of(me * 8, 8), 8), :]

    def send_fresh(index, carry):
        owner_row, part = index // 2, lax.rem(index, 2)
        owner_kv = index

        @pl.when(jnp.logical_not((owner_row == row) & (owner_kv == kv)))
        def _():
            pltpu.make_async_remote_copy(
                src_ref=sf.at[part, pl.ds(pl.multiple_of(owner_row * kv_size, 8), kv_size), :],
                dst_ref=rf.at[me],
                send_sem=send_sems.at[9],
                recv_sem=recv_sems.at[9],
                device_id={"row": owner_row, "kv": owner_kv},
                device_id_type=MESH,
            ).start()

        return carry

    lax.fori_loop(0, 2 * row_size, send_fresh, 0)
    owns_fresh = kv // 2 == row
    fresh_part = lax.rem(kv, 2)
    lane_sign = jnp.where(iota((1, HEAD), 1) < HEAD // 2, -1.0, 1.0)
    angle = len_smem[pool_smem[me]].astype(F32) * frequency[...]
    cosine = jnp.cos(angle)
    sine = jnp.sin(angle) * lane_sign
    slots = kv_size
    limits = [len_smem[pool_smem[row * slots + slot]] for slot in range(slots)]
    arrived(1)
    mine = jnp.sum(r2[...], axis=0)
    mine = mine * cosine + pltpu.roll(mine, HEAD // 2, 1) * sine
    mine = jnp.concatenate([mine, jnp.zeros_like(mine)], axis=0).astype(BF16)

    s3[...] = mine
    r3[kv] = mine

    def query_copy(offset, target, index):
        return pltpu.make_async_remote_copy(
            src_ref=s3,
            dst_ref=r3.at[target],
            send_sem=send_sems.at[2],
            recv_sem=query_sems.at[index],
            device_id={"kv": lax.rem(kv + offset, kv_size)},
            device_id_type=MESH,
        )

    for index in range(kv_size - 1):
        offset = (4, 3, 5, 2, 6, 1, 7)[index]
        query_copy(offset, kv, kv_size - offset).start()
    sent.append(2)

    @pl.when(owns_fresh)
    def _():
        rf[me] = sf[fresh_part, pl.ds(pl.multiple_of(row * kv_size, 8), kv_size), :]
        column = jnp.zeros((slots, HEAD), jnp.int32)
        for slot in range(slots):
            column = jnp.where(iota((slots, HEAD), 0) == slot, limits[slot], column)
        angles = column.astype(F32) * frequency[...]
        cosines = jnp.where(fresh_part == 0, jnp.cos(angles), 1.0)
        sines = jnp.where(fresh_part == 0, jnp.sin(angles) * lane_sign, 0.0)
        whole(9, rf.at[pl.ds(0, plane - 1)]).wait_recv()
        fresh = jnp.sum(rf[...], axis=0)
        fresh = fresh * cosines + pltpu.roll(fresh, HEAD // 2, 1) * sines
        fresh = jnp.concatenate([fresh, jnp.zeros_like(fresh)], axis=0).astype(BF16)
        sp[...] = fresh
        rp[fresh_part] = fresh

        def share(step, carry):
            pltpu.make_async_remote_copy(
                src_ref=sp,
                dst_ref=rp.at[fresh_part],
                send_sem=send_sems.at[10],
                recv_sem=recv_sems.at[10],
                device_id={"kv": lax.rem(kv + step, kv_size)},
                device_id_type=MESH,
            ).start()
            return carry

        lax.fori_loop(1, kv_size, share, 0)

    need("keys", "values")
    block = keys_v.shape[1]
    score_scale = HEAD ** (-0.5)
    position = kv * block + iota((GROUP, block), 1)
    lane = iota((GROUP, HEAD), 1)
    for group in ((0,), (1, 7), (2, 6), (4, 3, 5)):
        at = [lax.rem(kv + offset, kv_size) for offset in group]
        for offset, slot in zip(group, at):
            if offset:
                query_copy(offset, slot, offset).wait_recv()
        scores = [
            lax.dot_general(
                r3[slot, :GROUP, :],
                keys_v[slot],
                (((1,), (1,)), ((), ())),
                preferred_element_type=F32,
            )
            * score_scale
            for slot in at
        ]
        results = []
        for slot, score in zip(at, scores):
            limit = len_smem[pool_smem[row * slots + slot]]
            score = jnp.where(position < limit, score, FLOOR)
            peak = jnp.maximum(jnp.max(score, axis=1, keepdims=True), 0.1 * FLOOR)
            weights = jnp.exp(score - peak)
            total = jnp.sum(weights, axis=1, keepdims=True)
            product = jnp.dot(weights.astype(BF16), values_v[slot], preferred_element_type=F32)
            results.append((product, jnp.where(lane == 0, peak, total)))
        for offset, slot, (product, stats) in zip(group, at, results):
            place = slot // quarter * kv_size + kv
            s4[slot, :GROUP] = product
            s4[slot, GROUP:] = stats
            for target in (offset, (offset + quarter) % kv_size):
                if target == 0:
                    r4[place] = s4[slot]
                else:
                    pltpu.make_async_remote_copy(
                        src_ref=s4.at[slot],
                        dst_ref=r4.at[place],
                        send_sem=send_sems.at[3],
                        recv_sem=recv_sems.at[3],
                        device_id={"kv": lax.rem(kv + target, kv_size)},
                        device_id_type=MESH,
                    ).start()
    sent.append(3)

    @pl.when(owns_fresh)
    def _():
        whole(10, rp.at[0]).wait_recv()

    @pl.when(jnp.logical_not(owns_fresh))
    def _():
        whole(10, rp).wait_recv()

    new_keys[...] = rp[0][:slots]
    new_values[...] = rp[1][:slots]
    fresh_keys = rp[0].astype(F32)
    fresh_values = rp[1].astype(F32)
    fresh = []
    for which in range(2):
        slot = lax.rem(kv, quarter) + quarter * which
        this_slot = iota((16, HEAD), 0) == slot
        fresh_key = jnp.sum(jnp.where(this_slot, fresh_keys, 0.0), axis=0, keepdims=True)
        fresh_value = jnp.sum(jnp.where(this_slot, fresh_values, 0.0), axis=0, keepdims=True)
        fresh_query = r3[slot].astype(F32)[:GROUP]
        fresh_score = jnp.sum(fresh_query * fresh_key, axis=1, keepdims=True) * score_scale
        fresh.append((fresh_score, fresh_value))
    arrived(3)
    mixed = []
    for which, (fresh_score, fresh_value) in enumerate(fresh):
        parts = r4[which * kv_size : (which + 1) * kv_size]
        peaks = [parts[source, GROUP:, 0:1] for source in range(slots)]
        joint = fresh_score
        for peak in peaks:
            joint = jnp.maximum(joint, peak)
        fresh_weight = jnp.exp(fresh_score - joint)
        total = fresh_weight
        numer = fresh_weight.astype(BF16).astype(F32) * fresh_value
        for source in range(slots):
            fade = jnp.exp(peaks[source] - joint)
            total = total + parts[source, GROUP:, 1:2] * fade
            numer = numer + parts[source, :GROUP] * fade
        mixed.append(numer / total)
    mixed = jnp.concatenate(mixed, axis=0).astype(BF16)

    pair = row * quarter + lax.rem(kv, quarter)
    s5[...] = mixed
    r5[pair] = mixed
    for kv_step, row_step in (
        (2, 2), (2, 1), (2, 3), (7, 2), (1, 2), (2, 0), (7, 1), (7, 3),
        (1, 1), (1, 3), (0, 2), (7, 0), (1, 0), (0, 1), (0, 3),
    ):
        pltpu.make_async_remote_copy(
            src_ref=s5,
            dst_ref=r5.at[pair],
            send_sem=send_sems.at[4],
            recv_sem=recv_sems.at[4],
            device_id={
                "row": lax.rem(row + row_step, row_size),
                "kv": lax.rem(kv + kv_step, kv_size),
            },
            device_id_type=MESH,
        ).start()
    sent.append(4)
    need("out")
    arrived(4)
    w8[...] = r5[...].astype(F32).reshape(w8.shape)
    mixed_all = jnp.concatenate(
        [w8[pl.ds(head, seqs, stride=8), :].astype(BF16) for head in range(GROUP)], axis=1
    )
    projected = jnp.dot(mixed_all, out_v[...], preferred_element_type=F32)

    half = seqs // 2
    half_rows = row_size // 2
    my_block = row // half_rows

    projected = projected.astype(BF16)
    for block, phase in enumerate((5, 11)):
        part = projected[block * half : (block + 1) * half]
        s6[block] = part
        r6[block, tp] = part
        send_tp(phase, s6.at[block], r6.at[block, tp])
    need("ffn", "gate", "up")
    ffn = ffn_gain[...].astype(F32).reshape(1, width)
    blank = jnp.zeros((half, HEAD), F32)
    chunks = gate_v.shape[1] // HEAD
    streams = []
    for block, phase in enumerate((5, 11)):
        arrived(phase)
        total = r6[block, 0].astype(F32)
        for source in range(1, tp_size):
            total = total + r6[block, source].astype(F32)
        rows = (stream_pairs[block * half : (block + 1) * half] + total).astype(BF16).astype(F32)
        streams.append(rows)
        square_column = jnp.broadcast_to(
            jnp.sum(rows * rows, axis=1, keepdims=True), (half, HEAD)
        )
        scaled = (rows * ffn).astype(BF16)

        gate = jnp.dot(scaled, gate_v[...], preferred_element_type=F32)
        up = jnp.dot(scaled, up_v[...], preferred_element_type=F32)
        base = block * half * 32
        for part in range(chunks):
            columns = slice(part * HEAD, (part + 1) * HEAD)
            w7[pl.ds(base + part, half, stride=32), :] = gate[:, columns]
            w7[pl.ds(base + part + 16, half, stride=32), :] = up[:, columns]
        high = square_column.astype(BF16).astype(F32)
        w7[pl.ds(base + 14, half, stride=32), :] = high
        w7[pl.ds(base + 15, half, stride=32), :] = square_column - high
        w7[pl.ds(base + 30, half, stride=32), :] = blank
        w7[pl.ds(base + 31, half, stride=32), :] = blank
        s7[base : base + half * 32, :] = w7[base : base + half * 32, :].astype(BF16)

        def send_partial(index, carry, block=block):
            other_row = block * half_rows + lax.rem(index, half_rows)
            other_kv = lax.rem(kv + far_first(index // half_rows, kv_size), kv_size)
            other = other_row * kv_size + other_kv

            @pl.when(other != me)
            def _():
                pltpu.make_async_remote_copy(
                    src_ref=s7.at[pl.ds(pl.multiple_of(other * 32, 32), 32), :],
                    dst_ref=r7.at[me],
                    send_sem=send_sems.at[6],
                    recv_sem=recv_sems.at[6],
                    device_id={"row": other_row, "kv": other_kv},
                    device_id_type=MESH,
                ).start()

            return carry

        lax.fori_loop(0, half, send_partial, 0)
    sent.append(6)
    r7[me] = s7[pl.ds(pl.multiple_of(me * 32, 32), 32), :]
    need("down")
    arrived(6)
    sums = jnp.sum(r7[...].astype(F32), axis=0)
    scale = lax.rsqrt((sums[14:15] + sums[15:16]) / D + EPSILON)
    gate = sums[:16] * scale
    up = sums[16:] * scale
    activated = (gate / (1.0 + jnp.exp(-gate)) * up).astype(BF16)

    s8[...] = activated
    r8[me] = activated
    def share_activated(index, carry):
        other_row, other_kv = plane_partner(index)
        pltpu.make_async_remote_copy(
            src_ref=s8,
            dst_ref=r8.at[me],
            send_sem=send_sems.at[7],
            recv_sem=recv_sems.at[7 + 6 * my_block],
            device_id={"row": other_row, "kv": other_kv},
            device_id_type=MESH,
        ).start()
        return carry

    lax.fori_loop(0, plane - 1, share_activated, 0)
    sent.append(7)
    for block, phase in enumerate((8, 12)):

        @pl.when(my_block == block)
        def _(block=block):
            whole(7 + 6 * block, r8.at[pl.ds(0, half - 1)]).wait_recv()

        @pl.when(my_block != block)
        def _(block=block):
            whole(7 + 6 * block, r8.at[pl.ds(0, half)]).wait_recv()

        w8[...] = r8[block * half : (block + 1) * half].astype(F32).reshape(w8.shape)
        active = jnp.concatenate(
            [w8[pl.ds(part, half, stride=16), :].astype(BF16) for part in range(chunks)], axis=1
        )
        down = jnp.dot(active, down_v[...], preferred_element_type=F32).astype(BF16)

        s9[block] = down
        r9[block, tp] = down
        send_tp(phase, s9.at[block], r9.at[block, tp])
    results = []
    for block, phase in enumerate((8, 12)):
        arrived(phase)
        total = r9[block, 0].astype(F32)
        for source in range(1, tp_size):
            total = total + r9[block, source].astype(F32)
        results.append((streams[block] + total).astype(BF16))
    result = jnp.concatenate(results, axis=0)
    layer_out[...] = jnp.dot(to_seqs, result, preferred_element_type=F32).astype(BF16)
    drain()


def hand_out(result, keys, values, layer_out, new_keys, new_values, sems):
    copies = [
        pltpu.make_async_copy(result, layer_out, sems.at[0]),
        pltpu.make_async_copy(keys, new_keys, sems.at[1]),
        pltpu.make_async_copy(values, new_values, sems.at[2]),
    ]
    for copy in copies:
        copy.start()
    for copy in copies:
        copy.wait()


def local(
    sizes,
    tokens,
    attn_gain,
    w_qkv,
    w_out,
    ffn_gain,
    w_gate,
    w_up,
    w_down,
    cache_keys,
    cache_values,
    cache_len,
    pool_seq,
):
    tp_size, row_size, kv_size = sizes
    seqs, width = tokens.shape
    pair = np.arange(HEAD) % (HEAD // 2)
    frequency = (ROPE_BASE ** (-2.0 * pair / HEAD)).astype(np.float32).reshape(1, HEAD)
    plane = row_size * kv_size
    vmem = pl.BlockSpec(memory_space=pltpu.VMEM)
    hbm = pl.BlockSpec(memory_space=pltpu.HBM)
    scratch = [
        pltpu.VMEM((1, HEAD), F32),
        pltpu.SMEM(pool_seq.shape, jnp.int32),
        pltpu.SMEM(cache_len.shape, jnp.int32),
        pltpu.VMEM(tokens.shape, BF16),
        pltpu.VMEM(attn_gain.shape, BF16),
        pltpu.VMEM(ffn_gain.shape, BF16),
        pltpu.VMEM(w_qkv.shape, BF16),
        pltpu.VMEM(w_out.shape, BF16),
        pltpu.VMEM(w_gate.shape, BF16),
        pltpu.VMEM(w_up.shape, BF16),
        pltpu.VMEM(w_down.shape, BF16),
        pltpu.VMEM(cache_keys.shape, BF16),
        pltpu.VMEM(cache_values.shape, BF16),
        pltpu.VMEM((1, 1, HEAD), F32),
        pltpu.VMEM((plane, 1, HEAD), F32),
        pltpu.VMEM((plane * 8, HEAD), F32),
        pltpu.VMEM((plane, 8, HEAD), F32),
        pltpu.VMEM((2, plane, HEAD), F32),
        pltpu.VMEM((plane, 8, HEAD), F32),
        pltpu.VMEM((16, HEAD), BF16),
        pltpu.VMEM((kv_size, 16, HEAD), BF16),
        pltpu.VMEM((16, HEAD), BF16),
        pltpu.VMEM((2, 16, HEAD), BF16),
        pltpu.VMEM((kv_size, 16, HEAD), F32),
        pltpu.VMEM((2 * kv_size, 16, HEAD), F32),
        pltpu.VMEM((16, HEAD), BF16),
        pltpu.VMEM((plane // 2, 16, HEAD), BF16),
        pltpu.VMEM((2, seqs // 2, width), BF16),
        pltpu.VMEM((2, tp_size, seqs // 2, width), BF16),
        pltpu.VMEM((plane * 32, HEAD), F32),
        pltpu.VMEM((plane * 32, HEAD), BF16),
        pltpu.VMEM((plane, 32, HEAD), BF16),
        pltpu.VMEM((16, HEAD), BF16),
        pltpu.VMEM((plane, 16, HEAD), BF16),
        pltpu.VMEM((plane * 8, HEAD), F32),
        pltpu.VMEM((2, seqs // 2, width), BF16),
        pltpu.VMEM((2, tp_size, seqs // 2, width), BF16),
        pltpu.SemaphoreType.DMA((13,)),
        pltpu.SemaphoreType.DMA((14,)),
        pltpu.SemaphoreType.DMA((14,)),
        pltpu.SemaphoreType.DMA((kv_size,)),
    ]
    result, keys, values = pl.pallas_call(
        functools.partial(kernel, tp_size, row_size, kv_size),
        out_shape=(
            jax.ShapeDtypeStruct((seqs, width), BF16),
            jax.ShapeDtypeStruct((kv_size, HEAD), BF16),
            jax.ShapeDtypeStruct((kv_size, HEAD), BF16),
        ),
        in_specs=[hbm] * 13,
        out_specs=(vmem, vmem, vmem),
        scratch_shapes=scratch,
        compiler_params=pltpu.CompilerParams(
            collective_id=0, has_side_effects=True, vmem_limit_bytes=24 * 1024 * 1024
        ),
    )(
        *(
            pltpu.with_memory_space_constraint(part, pltpu.HBM)
            for part in (
                frequency,
                pool_seq,
                cache_len,
                tokens,
                attn_gain,
                ffn_gain,
                w_qkv,
                w_out,
                w_gate,
                w_up,
                w_down,
                cache_keys,
                cache_values,
            )
        )
    )
    return pl.pallas_call(
        hand_out,
        out_shape=(
            jax.ShapeDtypeStruct((seqs, width), BF16),
            jax.ShapeDtypeStruct((kv_size, HEAD), BF16),
            jax.ShapeDtypeStruct((kv_size, HEAD), BF16),
        ),
        in_specs=[vmem] * 3,
        out_specs=(hbm, hbm, hbm),
        scratch_shapes=[pltpu.SemaphoreType.DMA((3,))],
    )(*(pltpu.with_memory_space_constraint(part, pltpu.VMEM) for part in (result, keys, values)))


def solution(mesh):
    sizes = (mesh.shape["tp"], mesh.shape["row"], mesh.shape["kv"])
    return jax.shard_map(
        functools.partial(local, sizes),
        mesh=mesh,
        in_specs=(
            P(None, ("row", "kv")),
            P(("row", "kv")),
            P(("row", "kv"), "tp"),
            P("tp", ("row", "kv")),
            P(("row", "kv")),
            P(("row", "kv"), "tp"),
            P(("row", "kv"), "tp"),
            P("tp", ("row", "kv")),
            P("row", "kv", "tp"),
            P("row", "kv", "tp"),
            P(),
            P(),
        ),
        out_specs=(P(None, ("row", "kv")), P("row", "tp"), P("row", "tp")),
        check_vma=False,
    )
```

```python
import functools

import jax
import jax.numpy as jnp
import numpy as np
from jax import lax
from jax.experimental import pallas as pl
from jax.experimental.pallas import tpu as pltpu
from jax.sharding import PartitionSpec as P

D = 8192
HEAD = 128
GROUP = 8
EPSILON = 1e-05
ROPE_BASE = 500000.0
FLOOR = -1e30
MESH = pl.DeviceIdType.MESH
F32 = jnp.float32
BF16 = jnp.bfloat16


def iota(shape, dim):
    return lax.broadcasted_iota(jnp.int32, shape, dim)


def far_first(index, size):
    half = (index + 1) // 2
    return size // 2 + (1 - 2 * lax.rem(index, 2)) * half


def kernel(
    tp_size,
    row_size,
    kv_size,
    frequency_hbm,
    pool_hbm,
    len_hbm,
    tokens_hbm,
    attn_hbm,
    ffn_hbm,
    w_qkv,
    w_out,
    w_gate,
    w_up,
    w_down,
    cache_keys,
    cache_values,
    layer_out,
    new_keys,
    new_values,
    frequency,
    pool_smem,
    len_smem,
    tokens,
    attn_gain,
    ffn_gain,
    qkv_v,
    out_v,
    gate_v,
    up_v,
    down_v,
    keys_v,
    values_v,
    turned_keys,
    s1,
    r1,
    s2,
    r2,
    sf,
    rf,
    s3,
    r3,
    sp,
    rp,
    s4,
    r4,
    s5,
    r5,
    s6,
    r6,
    w7,
    s7,
    r7,
    s8,
    r8,
    w8,
    s9,
    r9,
    load_sems,
    send_sems,
    recv_sems,
    query_sems,
):
    plane = row_size * kv_size
    tp = lax.axis_index("tp")
    row = lax.axis_index("row")
    kv = lax.axis_index("kv")
    me = row * kv_size + kv

    barrier = pltpu.get_barrier_semaphore()

    def plane_partner(index):
        other_row = lax.rem(row + far_first(lax.rem(index, row_size), row_size), row_size)
        other_kv = lax.rem(kv + far_first(index // row_size, kv_size), kv_size)
        return other_row, other_kv

    def greet_plane(index, carry):
        other_row, other_kv = plane_partner(index)
        pl.semaphore_signal(
            barrier,
            inc=1,
            device_id={"row": other_row, "kv": other_kv},
            device_id_type=MESH,
        )
        return carry

    def greet_tp(step, carry):
        pl.semaphore_signal(
            barrier, inc=1, device_id={"tp": lax.rem(tp + step, tp_size)}, device_id_type=MESH
        )
        return carry

    lax.fori_loop(0, plane - 1, greet_plane, 0)
    lax.fori_loop(1, tp_size, greet_tp, 0)

    pending = {}
    for index, (name, source, target) in enumerate(
        (
            ("pool", pool_hbm, pool_smem),
            ("tokens", tokens_hbm, tokens),
            ("len", len_hbm, len_smem),
            ("attn", attn_hbm, attn_gain),
            ("frequency", frequency_hbm, frequency),
            ("qkv", w_qkv, qkv_v),
            ("keys", cache_keys, keys_v),
            ("values", cache_values, values_v),
            ("out", w_out, out_v),
            ("ffn", ffn_hbm, ffn_gain),
            ("gate", w_gate, gate_v),
            ("up", w_up, up_v),
            ("down", w_down, down_v),
        )
    ):
        pending[name] = pltpu.make_async_copy(source, target, load_sems.at[index])
        pending[name].start()

    def need(*names):
        for name in names:
            pending.pop(name).wait()

    sent = []

    def send_plane(phase, source, target):
        sent.append(phase)

        def one(index, carry):
            other_row, other_kv = plane_partner(index)
            pltpu.make_async_remote_copy(
                src_ref=source(other_row * kv_size + other_kv),
                dst_ref=target,
                send_sem=send_sems.at[phase],
                recv_sem=recv_sems.at[phase],
                device_id={"row": other_row, "kv": other_kv},
                device_id_type=MESH,
            ).start()
            return carry

        lax.fori_loop(0, plane - 1, one, 0)

    def send_tp(phase, source, target):
        sent.append(phase)

        def one(index, carry):
            pltpu.make_async_remote_copy(
                src_ref=source,
                dst_ref=target,
                send_sem=send_sems.at[phase],
                recv_sem=recv_sems.at[phase],
                device_id={"tp": lax.rem(tp + far_first(index, tp_size), tp_size)},
                device_id_type=MESH,
            ).start()
            return carry

        lax.fori_loop(0, tp_size - 1, one, 0)

    def whole(phase, part):
        return pltpu.make_async_remote_copy(
            src_ref=part,
            dst_ref=part,
            send_sem=send_sems.at[phase],
            recv_sem=recv_sems.at[phase],
            device_id={"tp": tp},
            device_id_type=MESH,
        )

    others = {
        0: r1.at[pl.ds(0, plane - 1)],
        1: r2.at[pl.ds(0, plane - 1)],
        2: r3.at[pl.ds(0, kv_size - 1)],
        3: r4.at[pl.ds(0, 2 * (kv_size - 1))],
        4: r5.at[pl.ds(0, plane // 2 - 1)],
        5: r6.at[0, pl.ds(0, tp_size - 1)],
        11: r6.at[1, pl.ds(0, tp_size - 1)],
        6: r7.at[pl.ds(0, plane - 1)],
        7: r8.at[pl.ds(0, plane - 1)],
        8: r9.at[0, pl.ds(0, tp_size - 1)],
        12: r9.at[1, pl.ds(0, tp_size - 1)],
    }

    def drain():
        for phase in sent:
            whole(phase, others[phase]).wait_send()

        if 1 in sent:
            @pl.when(owns_fresh)
            def _():
                whole(9, rf.at[pl.ds(0, row_size - 1)]).wait_send()

            @pl.when(jnp.logical_not(owns_fresh))
            def _():
                whole(9, rf.at[pl.ds(0, row_size)]).wait_send()

        if 2 in sent:
            @pl.when(owns_fresh)
            def _():
                whole(10, r3.at[pl.ds(0, kv_size - 1)]).wait_send()

    def arrived(phase):
        whole(phase, others[phase]).wait_recv()

    seqs = tokens.shape[0]
    width = tokens.shape[1]
    need("pool", "tokens")
    holder = jnp.zeros((seqs, seqs), jnp.int32)
    for slot in range(seqs):
        holder = jnp.where(iota((seqs, seqs), 0) == slot, pool_smem[slot], holder)
    to_slots = (holder == iota((seqs, seqs), 1)).astype(BF16)
    stream = jnp.dot(to_slots, tokens[...], preferred_element_type=F32)
    quarter = kv_size // 2
    holder = jnp.zeros((seqs, seqs), jnp.int32)
    held = jnp.zeros((seqs, seqs), jnp.int32)
    for index in range(seqs):
        group, place = index // kv_size, index % kv_size
        seq = pool_smem[group * kv_size + place // 2 + quarter * (place % 2)]
        holder = jnp.where(iota((seqs, seqs), 0) == index, seq, holder)
        held = jnp.where(iota((seqs, seqs), 1) == index, seq, held)
    to_pairs = (holder == iota((seqs, seqs), 1)).astype(BF16)
    to_seqs = (held == iota((seqs, seqs), 0)).astype(BF16)
    stream_pairs = jnp.dot(to_pairs, tokens[...], preferred_element_type=F32)

    wide = iota((seqs, HEAD), 0) == iota((seqs, HEAD), 1)

    def as_lanes(column):
        return jnp.sum(
            jnp.where(wide, jnp.broadcast_to(column, (seqs, HEAD)), 0.0), axis=0, keepdims=True
        )

    def as_column(lanes):
        return jnp.sum(
            jnp.where(wide, jnp.broadcast_to(lanes, (seqs, HEAD)), 0.0), axis=1, keepdims=True
        )

    squares = as_lanes(jnp.sum(stream * stream, axis=1, keepdims=True))
    s1[0] = squares
    r1[me] = squares

    pl.semaphore_wait(barrier, plane - 1 + tp_size - 1)

    send_plane(0, lambda other: s1.at[0], r1.at[me])
    arrived(0)
    first_sum = as_column(jnp.sum(r1[...], axis=0))
    need("attn", "len", "frequency", "qkv")
    gain = attn_gain[...].astype(F32).reshape(1, width)
    normed = (stream * lax.rsqrt(first_sum / D + EPSILON) * gain).astype(BF16)

    united = jnp.dot(normed, qkv_v[...], preferred_element_type=F32)
    for part in range(GROUP):
        s2[pl.ds(part, seqs, stride=GROUP), :] = united[:, part * HEAD : (part + 1) * HEAD]
    fresh = united[:, GROUP * HEAD :].astype(BF16).astype(F32)
    for group in range(row_size):
        rows = slice(group * kv_size, (group + 1) * kv_size)
        sf[group] = jnp.concatenate(
            [fresh[rows, :HEAD], fresh[rows, HEAD:]], axis=0
        ).astype(BF16)
    send_plane(1, lambda other: s2.at[pl.ds(pl.multiple_of(other * 8, 8), 8), :], r2.at[me])
    r2[me] = s2[pl.ds(pl.multiple_of(me * 8, 8), 8), :]

    def send_fresh(index, carry):
        @pl.when(jnp.logical_not((index == row) & (2 * index == kv)))
        def _():
            pltpu.make_async_remote_copy(
                src_ref=sf.at[index],
                dst_ref=rf.at[me],
                send_sem=send_sems.at[9],
                recv_sem=recv_sems.at[9],
                device_id={"row": index, "kv": 2 * index},
                device_id_type=MESH,
            ).start()

        return carry

    lax.fori_loop(0, row_size, send_fresh, 0)
    owns_fresh = kv == 2 * row
    lane_sign = jnp.where(iota((1, HEAD), 1) < HEAD // 2, -1.0, 1.0)
    angle = len_smem[pool_smem[me]].astype(F32) * frequency[...]
    cosine = jnp.cos(angle)
    sine = jnp.sin(angle) * lane_sign
    slots = kv_size
    column = jnp.zeros((2 * slots, HEAD), jnp.int32)
    for slot in range(slots):
        limit = len_smem[pool_smem[row * slots + slot]]
        column = jnp.where(iota((2 * slots, HEAD), 0) == slot, limit, column)
    angles = column.astype(F32) * frequency[...]
    turned = iota((2 * slots, HEAD), 0) < slots
    cosines = jnp.where(turned, jnp.cos(angles), 1.0)
    sines = jnp.where(turned, jnp.sin(angles) * lane_sign, 0.0)
    need("keys")
    for slot in range(slots):
        turned_keys[slot] = keys_v[slot].T
    arrived(1)
    mine = jnp.sum(r2[...], axis=0)
    mine = mine * cosine + pltpu.roll(mine, HEAD // 2, 1) * sine
    mine = jnp.concatenate([mine, jnp.zeros_like(mine)], axis=0).astype(BF16)

    s3[...] = mine
    r3[kv] = mine

    def query_copy(offset, target, index):
        return pltpu.make_async_remote_copy(
            src_ref=s3,
            dst_ref=r3.at[target],
            send_sem=send_sems.at[2],
            recv_sem=query_sems.at[index],
            device_id={"kv": lax.rem(kv + offset, kv_size)},
            device_id_type=MESH,
        )

    for index in range(kv_size - 1):
        offset = (4, 3, 5, 2, 6, 1, 7)[index]
        query_copy(offset, kv, kv_size - offset).start()
    sent.append(2)

    @pl.when(owns_fresh)
    def _():
        rf[me] = sf[row]
        whole(9, rf.at[pl.ds(0, plane - 1)]).wait_recv()
        fresh = jnp.sum(rf[...].astype(F32), axis=0)
        fresh = fresh * cosines + pltpu.roll(fresh, HEAD // 2, 1) * sines
        sp[...] = fresh.astype(BF16)
        rp[...] = fresh.astype(BF16)

        def share(step, carry):
            pltpu.make_async_remote_copy(
                src_ref=sp,
                dst_ref=rp,
                send_sem=send_sems.at[10],
                recv_sem=recv_sems.at[10],
                device_id={"kv": lax.rem(kv + step, kv_size)},
                device_id_type=MESH,
            ).start()
            return carry

        lax.fori_loop(1, kv_size, share, 0)

    need("values")
    block = keys_v.shape[1]
    score_scale = HEAD ** (-0.5)
    position = kv * block + iota((GROUP, block), 1)
    lane = iota((GROUP, HEAD), 1)
    for group in ((0,), (1, 7), (2, 6, 3, 5), (4,)):
        at = [lax.rem(kv + offset, kv_size) for offset in group]
        for offset, slot in zip(group, at):
            if offset:
                query_copy(offset, slot, offset).wait_recv()
        scores = [
            lax.dot_general(
                r3[slot, :GROUP, :],
                turned_keys[slot],
                (((1,), (0,)), ((), ())),
                preferred_element_type=F32,
            )
            * score_scale
            for slot in at
        ]
        results = []
        for slot, score in zip(at, scores):
            limit = len_smem[pool_smem[row * slots + slot]]
            score = jnp.where(position < limit, score, FLOOR)
            peak = jnp.maximum(jnp.max(score, axis=1, keepdims=True), 0.1 * FLOOR)
            weights = jnp.exp(score - peak)
            total = jnp.sum(weights, axis=1, keepdims=True)
            product = jnp.dot(weights.astype(BF16), values_v[slot], preferred_element_type=F32)
            results.append((product, jnp.where(lane == 0, peak, total)))
        for offset, slot, (product, stats) in zip(group, at, results):
            place = slot // quarter * kv_size + kv
            s4[slot, :GROUP] = product
            s4[slot, GROUP:] = stats
            for target in ((offset + 2) % kv_size, (offset + 2 + quarter) % kv_size):
                if target == 0:
                    r4[place] = s4[slot]
                else:
                    pltpu.make_async_remote_copy(
                        src_ref=s4.at[slot],
                        dst_ref=r4.at[place],
                        send_sem=send_sems.at[3],
                        recv_sem=recv_sems.at[3],
                        device_id={"kv": lax.rem(kv + target, kv_size)},
                        device_id_type=MESH,
                    ).start()
    sent.append(3)

    @pl.when(jnp.logical_not(owns_fresh))
    def _():
        whole(10, rp).wait_recv()

    fresh = rp[...].astype(F32)
    fresh_keys, fresh_values = fresh[:slots], fresh[slots:]
    new_keys[...] = fresh_keys.astype(BF16)
    new_values[...] = fresh_values.astype(BF16)
    fresh = []
    for which in range(2):
        slot = lax.rem(kv + 2, quarter) + quarter * which
        this_slot = iota((slots, HEAD), 0) == slot
        fresh_key = jnp.sum(jnp.where(this_slot, fresh_keys, 0.0), axis=0, keepdims=True)
        fresh_value = jnp.sum(jnp.where(this_slot, fresh_values, 0.0), axis=0, keepdims=True)
        fresh_query = r3[slot].astype(F32)[:GROUP]
        fresh_score = jnp.sum(fresh_query * fresh_key, axis=1, keepdims=True) * score_scale
        fresh.append((fresh_score, fresh_value))
    arrived(3)
    mixed = []
    for which, (fresh_score, fresh_value) in enumerate(fresh):
        parts = r4[which * kv_size : (which + 1) * kv_size]
        peaks = [parts[source, GROUP:, 0:1] for source in range(slots)]
        joint = fresh_score
        for peak in peaks:
            joint = jnp.maximum(joint, peak)
        fresh_weight = jnp.exp(fresh_score - joint)
        total = fresh_weight
        numer = fresh_weight.astype(BF16).astype(F32) * fresh_value
        for source in range(slots):
            fade = jnp.exp(peaks[source] - joint)
            total = total + parts[source, GROUP:, 1:2] * fade
            numer = numer + parts[source, :GROUP] * fade
        mixed.append(numer / total)
    mixed = jnp.concatenate(mixed, axis=0).astype(BF16)

    pair = row * quarter + lax.rem(kv + 2, quarter)
    s5[...] = mixed
    r5[pair] = mixed
    for kv_step, row_step in (
        (2, 2), (2, 1), (2, 3), (7, 2), (1, 2), (2, 0), (7, 1), (7, 3),
        (1, 1), (1, 3), (0, 2), (7, 0), (1, 0), (0, 1), (0, 3),
    ):
        pltpu.make_async_remote_copy(
            src_ref=s5,
            dst_ref=r5.at[pair],
            send_sem=send_sems.at[4],
            recv_sem=recv_sems.at[4],
            device_id={
                "row": lax.rem(row + row_step, row_size),
                "kv": lax.rem(kv + kv_step, kv_size),
            },
            device_id_type=MESH,
        ).start()
    sent.append(4)
    need("out")
    arrived(4)
    w8[...] = r5[...].astype(F32).reshape(w8.shape)
    mixed_all = jnp.concatenate(
        [w8[pl.ds(head, seqs, stride=8), :].astype(BF16) for head in range(GROUP)], axis=1
    )
    projected = jnp.dot(mixed_all, out_v[...], preferred_element_type=F32)

    half = seqs // 2
    half_rows = row_size // 2
    my_block = row // half_rows

    projected = projected.astype(BF16)
    for block, phase in enumerate((5, 11)):
        part = projected[block * half : (block + 1) * half]
        s6[block] = part
        r6[block, tp] = part
        send_tp(phase, s6.at[block], r6.at[block, tp])
    need("ffn", "gate", "up")
    ffn = ffn_gain[...].astype(F32).reshape(1, width)
    blank = jnp.zeros((half, HEAD), F32)
    chunks = gate_v.shape[1] // HEAD
    streams = []
    for block, phase in enumerate((5, 11)):
        arrived(phase)
        total = r6[block, 0].astype(F32)
        for source in range(1, tp_size):
            total = total + r6[block, source].astype(F32)
        rows = (stream_pairs[block * half : (block + 1) * half] + total).astype(BF16).astype(F32)
        streams.append(rows)
        square_column = jnp.broadcast_to(
            jnp.sum(rows * rows, axis=1, keepdims=True), (half, HEAD)
        )
        scaled = (rows * ffn).astype(BF16)

        gate = jnp.dot(scaled, gate_v[...], preferred_element_type=F32)
        up = jnp.dot(scaled, up_v[...], preferred_element_type=F32)
        base = block * half * 32
        for part in range(chunks):
            columns = slice(part * HEAD, (part + 1) * HEAD)
            w7[pl.ds(base + part, half, stride=32), :] = gate[:, columns]
            w7[pl.ds(base + part + 16, half, stride=32), :] = up[:, columns]
        high = square_column.astype(BF16).astype(F32)
        w7[pl.ds(base + 14, half, stride=32), :] = high
        w7[pl.ds(base + 15, half, stride=32), :] = square_column - high
        w7[pl.ds(base + 30, half, stride=32), :] = blank
        w7[pl.ds(base + 31, half, stride=32), :] = blank
        s7[base : base + half * 32, :] = w7[base : base + half * 32, :].astype(BF16)

        def send_partial(index, carry, block=block):
            other_row = block * half_rows + lax.rem(index, half_rows)
            other_kv = lax.rem(kv + far_first(index // half_rows, kv_size), kv_size)
            other = other_row * kv_size + other_kv

            @pl.when(other != me)
            def _():
                pltpu.make_async_remote_copy(
                    src_ref=s7.at[pl.ds(pl.multiple_of(other * 32, 32), 32), :],
                    dst_ref=r7.at[me],
                    send_sem=send_sems.at[6],
                    recv_sem=recv_sems.at[6],
                    device_id={"row": other_row, "kv": other_kv},
                    device_id_type=MESH,
                ).start()

            return carry

        lax.fori_loop(0, half, send_partial, 0)
    sent.append(6)
    r7[me] = s7[pl.ds(pl.multiple_of(me * 32, 32), 32), :]
    need("down")
    arrived(6)
    sums = jnp.sum(r7[...].astype(F32), axis=0)
    scale = lax.rsqrt((sums[14:15] + sums[15:16]) / D + EPSILON)
    gate = sums[:16] * scale
    up = sums[16:] * scale
    activated = (gate / (1.0 + jnp.exp(-gate)) * up).astype(BF16)

    s8[...] = activated
    r8[me] = activated
    def share_activated(index, carry):
        other_row, other_kv = plane_partner(index)
        pltpu.make_async_remote_copy(
            src_ref=s8,
            dst_ref=r8.at[me],
            send_sem=send_sems.at[7],
            recv_sem=recv_sems.at[7 + 6 * my_block],
            device_id={"row": other_row, "kv": other_kv},
            device_id_type=MESH,
        ).start()
        return carry

    lax.fori_loop(0, plane - 1, share_activated, 0)
    sent.append(7)
    for block, phase in enumerate((8, 12)):

        @pl.when(my_block == block)
        def _(block=block):
            whole(7 + 6 * block, r8.at[pl.ds(0, half - 1)]).wait_recv()

        @pl.when(my_block != block)
        def _(block=block):
            whole(7 + 6 * block, r8.at[pl.ds(0, half)]).wait_recv()

        w8[...] = r8[block * half : (block + 1) * half].astype(F32).reshape(w8.shape)
        active = jnp.concatenate(
            [w8[pl.ds(part, half, stride=16), :].astype(BF16) for part in range(chunks)], axis=1
        )
        down = jnp.dot(active, down_v[...], preferred_element_type=F32).astype(BF16)

        s9[block] = down
        r9[block, tp] = down
        send_tp(phase, s9.at[block], r9.at[block, tp])
    results = []
    for block, phase in enumerate((8, 12)):
        arrived(phase)
        total = r9[block, 0].astype(F32)
        for source in range(1, tp_size):
            total = total + r9[block, source].astype(F32)
        results.append((streams[block] + total).astype(BF16))
    result = jnp.concatenate(results, axis=0)
    layer_out[...] = jnp.dot(to_seqs, result, preferred_element_type=F32).astype(BF16)
    drain()


def hand_out(result, keys, values, layer_out, new_keys, new_values, sems):
    copies = [
        pltpu.make_async_copy(result, layer_out, sems.at[0]),
        pltpu.make_async_copy(keys, new_keys, sems.at[1]),
        pltpu.make_async_copy(values, new_values, sems.at[2]),
    ]
    for copy in copies:
        copy.start()
    for copy in copies:
        copy.wait()


def local(
    sizes,
    tokens,
    attn_gain,
    w_qkv,
    w_out,
    ffn_gain,
    w_gate,
    w_up,
    w_down,
    cache_keys,
    cache_values,
    cache_len,
    pool_seq,
):
    tp_size, row_size, kv_size = sizes
    seqs, width = tokens.shape
    pair = np.arange(HEAD) % (HEAD // 2)
    frequency = (ROPE_BASE ** (-2.0 * pair / HEAD)).astype(np.float32).reshape(1, HEAD)
    plane = row_size * kv_size
    vmem = pl.BlockSpec(memory_space=pltpu.VMEM)
    hbm = pl.BlockSpec(memory_space=pltpu.HBM)
    scratch = [
        pltpu.VMEM((1, HEAD), F32),
        pltpu.SMEM(pool_seq.shape, jnp.int32),
        pltpu.SMEM(cache_len.shape, jnp.int32),
        pltpu.VMEM(tokens.shape, BF16),
        pltpu.VMEM(attn_gain.shape, BF16),
        pltpu.VMEM(ffn_gain.shape, BF16),
        pltpu.VMEM(w_qkv.shape, BF16),
        pltpu.VMEM(w_out.shape, BF16),
        pltpu.VMEM(w_gate.shape, BF16),
        pltpu.VMEM(w_up.shape, BF16),
        pltpu.VMEM(w_down.shape, BF16),
        pltpu.VMEM(cache_keys.shape, BF16),
        pltpu.VMEM(cache_values.shape, BF16),
        pltpu.VMEM((kv_size, HEAD, cache_keys.shape[1]), BF16),
        pltpu.VMEM((1, 1, HEAD), F32),
        pltpu.VMEM((plane, 1, HEAD), F32),
        pltpu.VMEM((plane * 8, HEAD), F32),
        pltpu.VMEM((plane, 8, HEAD), F32),
        pltpu.VMEM((row_size, 16, HEAD), BF16),
        pltpu.VMEM((plane, 16, HEAD), BF16),
        pltpu.VMEM((16, HEAD), BF16),
        pltpu.VMEM((kv_size, 16, HEAD), BF16),
        pltpu.VMEM((16, HEAD), BF16),
        pltpu.VMEM((16, HEAD), BF16),
        pltpu.VMEM((kv_size, 16, HEAD), F32),
        pltpu.VMEM((2 * kv_size, 16, HEAD), F32),
        pltpu.VMEM((16, HEAD), BF16),
        pltpu.VMEM((plane // 2, 16, HEAD), BF16),
        pltpu.VMEM((2, seqs // 2, width), BF16),
        pltpu.VMEM((2, tp_size, seqs // 2, width), BF16),
        pltpu.VMEM((plane * 32, HEAD), F32),
        pltpu.VMEM((plane * 32, HEAD), BF16),
        pltpu.VMEM((plane, 32, HEAD), BF16),
        pltpu.VMEM((16, HEAD), BF16),
        pltpu.VMEM((plane, 16, HEAD), BF16),
        pltpu.VMEM((plane * 8, HEAD), F32),
        pltpu.VMEM((2, seqs // 2, width), BF16),
        pltpu.VMEM((2, tp_size, seqs // 2, width), BF16),
        pltpu.SemaphoreType.DMA((13,)),
        pltpu.SemaphoreType.DMA((14,)),
        pltpu.SemaphoreType.DMA((14,)),
        pltpu.SemaphoreType.DMA((kv_size,)),
    ]
    result, keys, values = pl.pallas_call(
        functools.partial(kernel, tp_size, row_size, kv_size),
        out_shape=(
            jax.ShapeDtypeStruct((seqs, width), BF16),
            jax.ShapeDtypeStruct((kv_size, HEAD), BF16),
            jax.ShapeDtypeStruct((kv_size, HEAD), BF16),
        ),
        in_specs=[hbm] * 13,
        out_specs=(vmem, vmem, vmem),
        scratch_shapes=scratch,
        compiler_params=pltpu.CompilerParams(
            collective_id=0, has_side_effects=True, vmem_limit_bytes=24 * 1024 * 1024
        ),
    )(
        *(
            pltpu.with_memory_space_constraint(part, pltpu.HBM)
            for part in (
                frequency,
                pool_seq,
                cache_len,
                tokens,
                attn_gain,
                ffn_gain,
                w_qkv,
                w_out,
                w_gate,
                w_up,
                w_down,
                cache_keys,
                cache_values,
            )
        )
    )
    return pl.pallas_call(
        hand_out,
        out_shape=(
            jax.ShapeDtypeStruct((seqs, width), BF16),
            jax.ShapeDtypeStruct((kv_size, HEAD), BF16),
            jax.ShapeDtypeStruct((kv_size, HEAD), BF16),
        ),
        in_specs=[vmem] * 3,
        out_specs=(hbm, hbm, hbm),
        scratch_shapes=[pltpu.SemaphoreType.DMA((3,))],
    )(*(pltpu.with_memory_space_constraint(part, pltpu.VMEM) for part in (result, keys, values)))


def solution(mesh):
    sizes = (mesh.shape["tp"], mesh.shape["row"], mesh.shape["kv"])
    return jax.shard_map(
        functools.partial(local, sizes),
        mesh=mesh,
        in_specs=(
            P(None, ("row", "kv")),
            P(("row", "kv")),
            P(("row", "kv"), "tp"),
            P("tp", ("row", "kv")),
            P(("row", "kv")),
            P(("row", "kv"), "tp"),
            P(("row", "kv"), "tp"),
            P("tp", ("row", "kv")),
            P("row", "kv", "tp"),
            P("row", "kv", "tp"),
            P(),
            P(),
        ),
        out_specs=(P(None, ("row", "kv")), P("row", "tp"), P("row", "tp")),
        check_vma=False,
    )
```

```python
import functools

import jax
import jax.numpy as jnp
import numpy as np
from jax import lax
from jax.experimental import pallas as pl
from jax.experimental.pallas import tpu as pltpu
from jax.sharding import PartitionSpec as P

D = 8192
HEAD = 128
GROUP = 8
EPSILON = 1e-05
ROPE_BASE = 500000.0
FLOOR = -1e30
MESH = pl.DeviceIdType.MESH
F32 = jnp.float32
BF16 = jnp.bfloat16


def iota(shape, dim):
    return lax.broadcasted_iota(jnp.int32, shape, dim)


def far_first(index, size):
    half = (index + 1) // 2
    return size // 2 + (1 - 2 * lax.rem(index, 2)) * half


def kernel(
    tp_size,
    row_size,
    kv_size,
    frequency_hbm,
    pool_hbm,
    len_hbm,
    tokens_hbm,
    attn_hbm,
    ffn_hbm,
    w_qkv,
    w_out,
    w_gate,
    w_up,
    w_down,
    cache_keys,
    cache_values,
    layer_out,
    new_keys,
    new_values,
    frequency,
    pool_smem,
    len_smem,
    tokens,
    attn_gain,
    ffn_gain,
    qkv_v,
    out_v,
    gate_v,
    up_v,
    down_v,
    keys_v,
    values_v,
    turned_keys,
    s1,
    r1,
    s2,
    r2,
    sf,
    rf,
    s3,
    r3,
    sp,
    rp,
    s4,
    r4,
    s5,
    r5,
    s6,
    r6,
    w7,
    s7,
    r7,
    s8,
    r8,
    w8,
    s9,
    r9,
    load_sems,
    send_sems,
    recv_sems,
    query_sems,
):
    plane = row_size * kv_size
    tp = lax.axis_index("tp")
    row = lax.axis_index("row")
    kv = lax.axis_index("kv")
    me = row * kv_size + kv

    barrier = pltpu.get_barrier_semaphore()

    def plane_partner(index):
        other_row = lax.rem(row + far_first(lax.rem(index, row_size), row_size), row_size)
        other_kv = lax.rem(kv + far_first(index // row_size, kv_size), kv_size)
        return other_row, other_kv

    def greet_plane(index, carry):
        other_row, other_kv = plane_partner(index)
        pl.semaphore_signal(
            barrier,
            inc=1,
            device_id={"row": other_row, "kv": other_kv},
            device_id_type=MESH,
        )
        return carry

    def greet_tp(step, carry):
        pl.semaphore_signal(
            barrier, inc=1, device_id={"tp": lax.rem(tp + step, tp_size)}, device_id_type=MESH
        )
        return carry

    lax.fori_loop(0, plane - 1, greet_plane, 0)
    lax.fori_loop(1, tp_size, greet_tp, 0)

    pending = {}
    for index, (name, source, target) in enumerate(
        (
            ("pool", pool_hbm, pool_smem),
            ("tokens", tokens_hbm, tokens),
            ("len", len_hbm, len_smem),
            ("attn", attn_hbm, attn_gain),
            ("frequency", frequency_hbm, frequency),
            ("qkv", w_qkv, qkv_v),
            ("keys", cache_keys, keys_v),
            ("values", cache_values, values_v),
            ("out", w_out, out_v),
            ("ffn", ffn_hbm, ffn_gain),
            ("gate", w_gate, gate_v),
            ("up", w_up, up_v),
            ("down", w_down, down_v),
        )
    ):
        pending[name] = pltpu.make_async_copy(source, target, load_sems.at[index])
        if index < 8:
            pending[name].start()

    def need(*names):
        for name in names:
            pending.pop(name).wait()

    def send_plane(phase, source, target):
        def one(index, carry):
            other_row, other_kv = plane_partner(index)
            pltpu.make_async_remote_copy(
                src_ref=source(other_row * kv_size + other_kv),
                dst_ref=target,
                send_sem=send_sems.at[phase],
                recv_sem=recv_sems.at[phase],
                device_id={"row": other_row, "kv": other_kv},
                device_id_type=MESH,
            ).start()
            return carry

        lax.fori_loop(0, plane - 1, one, 0)

    def send_tp(phase, source, target):
        def one(index, carry):
            pltpu.make_async_remote_copy(
                src_ref=source,
                dst_ref=target,
                send_sem=send_sems.at[phase],
                recv_sem=recv_sems.at[phase],
                device_id={"tp": lax.rem(tp + far_first(index, tp_size), tp_size)},
                device_id_type=MESH,
            ).start()
            return carry

        lax.fori_loop(0, tp_size - 1, one, 0)

    def whole(phase, part):
        return pltpu.make_async_remote_copy(
            src_ref=part,
            dst_ref=part,
            send_sem=send_sems.at[phase],
            recv_sem=recv_sems.at[phase],
            device_id={"tp": tp},
            device_id_type=MESH,
        )

    others = {
        0: r1.at[pl.ds(0, plane - 1)],
        1: r2.at[pl.ds(0, plane - 1)],
        2: r3.at[pl.ds(0, kv_size - 1)],
        3: r4.at[pl.ds(0, 2 * (kv_size - 1))],
        4: r5.at[pl.ds(0, plane // 2 - 1)],
        5: r6.at[0, pl.ds(0, tp_size - 1)],
        11: r6.at[1, pl.ds(0, tp_size - 1)],
        6: r7.at[pl.ds(0, plane - 1)],
        7: r8.at[pl.ds(0, plane - 1)],
        8: r9.at[0, pl.ds(0, tp_size - 1)],
        12: r9.at[1, pl.ds(0, tp_size - 1)],
    }

    def drain(*phases):
        for phase in phases:
            whole(phase, others[phase]).wait_send()

    def drain_fresh():
        @pl.when(owns_fresh)
        def _():
            whole(9, rf.at[pl.ds(0, row_size - 1)]).wait_send()
            whole(10, r3.at[pl.ds(0, kv_size - 1)]).wait_send()

        @pl.when(jnp.logical_not(owns_fresh))
        def _():
            whole(9, rf.at[pl.ds(0, row_size)]).wait_send()

    def arrived(phase):
        whole(phase, others[phase]).wait_recv()

    seqs = tokens.shape[0]
    width = tokens.shape[1]
    need("pool", "tokens")
    holder = jnp.zeros((seqs, seqs), jnp.int32)
    for slot in range(seqs):
        holder = jnp.where(iota((seqs, seqs), 0) == slot, pool_smem[slot], holder)
    to_slots = (holder == iota((seqs, seqs), 1)).astype(BF16)
    stream = jnp.dot(to_slots, tokens[...], preferred_element_type=F32)
    quarter = kv_size // 2
    holder = jnp.zeros((seqs, seqs), jnp.int32)
    held = jnp.zeros((seqs, seqs), jnp.int32)
    for index in range(seqs):
        group, place = index // kv_size, index % kv_size
        seq = pool_smem[group * kv_size + place // 2 + quarter * (place % 2)]
        holder = jnp.where(iota((seqs, seqs), 0) == index, seq, holder)
        held = jnp.where(iota((seqs, seqs), 1) == index, seq, held)
    to_pairs = (holder == iota((seqs, seqs), 1)).astype(BF16)
    to_seqs = (held == iota((seqs, seqs), 0)).astype(BF16)
    stream_pairs = jnp.dot(to_pairs, tokens[...], preferred_element_type=F32)

    wide = iota((seqs, HEAD), 0) == iota((seqs, HEAD), 1)

    def as_lanes(column):
        return jnp.sum(
            jnp.where(wide, jnp.broadcast_to(column, (seqs, HEAD)), 0.0), axis=0, keepdims=True
        )

    def as_column(lanes):
        return jnp.sum(
            jnp.where(wide, jnp.broadcast_to(lanes, (seqs, HEAD)), 0.0), axis=1, keepdims=True
        )

    squares = as_lanes(jnp.sum(stream * stream, axis=1, keepdims=True))
    s1[0] = squares
    r1[me] = squares

    pl.semaphore_wait(barrier, plane - 1 + tp_size - 1)

    send_plane(0, lambda other: s1.at[0], r1.at[me])
    arrived(0)
    first_sum = as_column(jnp.sum(r1[...], axis=0))
    need("attn", "len", "frequency", "qkv")
    gain = attn_gain[...].astype(F32).reshape(1, width)
    normed = (stream * lax.rsqrt(first_sum / D + EPSILON) * gain).astype(BF16)

    united = jnp.dot(normed, qkv_v[...], preferred_element_type=F32)
    for part in range(GROUP):
        s2[pl.ds(part, seqs, stride=GROUP), :] = united[:, part * HEAD : (part + 1) * HEAD]
    fresh = united[:, GROUP * HEAD :].astype(BF16).astype(F32)
    for group in range(row_size):
        rows = slice(group * kv_size, (group + 1) * kv_size)
        sf[group] = jnp.concatenate(
            [fresh[rows, :HEAD], fresh[rows, HEAD:]], axis=0
        ).astype(BF16)
    send_plane(1, lambda other: s2.at[pl.ds(pl.multiple_of(other * 8, 8), 8), :], r2.at[me])
    r2[me] = s2[pl.ds(pl.multiple_of(me * 8, 8), 8), :]

    def send_fresh(index, carry):
        @pl.when(jnp.logical_not((index == row) & (2 * index == kv)))
        def _():
            pltpu.make_async_remote_copy(
                src_ref=sf.at[index],
                dst_ref=rf.at[me],
                send_sem=send_sems.at[9],
                recv_sem=recv_sems.at[9],
                device_id={"row": index, "kv": 2 * index},
                device_id_type=MESH,
            ).start()

        return carry

    lax.fori_loop(0, row_size, send_fresh, 0)
    owns_fresh = kv == 2 * row
    lane_sign = jnp.where(iota((1, HEAD), 1) < HEAD // 2, -1.0, 1.0)
    angle = len_smem[pool_smem[me]].astype(F32) * frequency[...]
    cosine = jnp.cos(angle)
    sine = jnp.sin(angle) * lane_sign
    slots = kv_size
    column = jnp.zeros((2 * slots, HEAD), jnp.int32)
    for slot in range(slots):
        limit = len_smem[pool_smem[row * slots + slot]]
        column = jnp.where(iota((2 * slots, HEAD), 0) == slot, limit, column)
    angles = column.astype(F32) * frequency[...]
    turned = iota((2 * slots, HEAD), 0) < slots
    cosines = jnp.where(turned, jnp.cos(angles), 1.0)
    sines = jnp.where(turned, jnp.sin(angles) * lane_sign, 0.0)
    for name in ("out", "ffn", "gate", "up", "down"):
        pending[name].start()
    need("keys")
    for slot in range(slots):
        turned_keys[slot] = keys_v[slot].T
    arrived(1)
    mine = jnp.sum(r2[...], axis=0)
    mine = mine * cosine + pltpu.roll(mine, HEAD // 2, 1) * sine
    mine = jnp.concatenate([mine, jnp.zeros_like(mine)], axis=0).astype(BF16)

    s3[...] = mine
    r3[kv] = mine

    def query_copy(offset, target, index):
        return pltpu.make_async_remote_copy(
            src_ref=s3,
            dst_ref=r3.at[target],
            send_sem=send_sems.at[2],
            recv_sem=query_sems.at[index],
            device_id={"kv": lax.rem(kv + offset, kv_size)},
            device_id_type=MESH,
        )

    for index in range(kv_size - 1):
        offset = (4, 3, 5, 2, 6, 1, 7)[index]
        query_copy(offset, kv, kv_size - offset).start()

    @pl.when(owns_fresh)
    def _():
        rf[me] = sf[row]
        whole(9, rf.at[pl.ds(0, plane - 1)]).wait_recv()
        fresh = jnp.sum(rf[...].astype(F32), axis=0)
        fresh = fresh * cosines + pltpu.roll(fresh, HEAD // 2, 1) * sines
        sp[...] = fresh.astype(BF16)
        rp[...] = fresh.astype(BF16)

        def share(step, carry):
            pltpu.make_async_remote_copy(
                src_ref=sp,
                dst_ref=rp,
                send_sem=send_sems.at[10],
                recv_sem=recv_sems.at[10],
                device_id={"kv": lax.rem(kv + step, kv_size)},
                device_id_type=MESH,
            ).start()
            return carry

        lax.fori_loop(1, kv_size, share, 0)

    need("values")
    block = keys_v.shape[1]
    score_scale = HEAD ** (-0.5)
    position = kv * block + iota((GROUP, block), 1)
    lane = iota((GROUP, HEAD), 1)
    for group in ((0,), (1, 7), (2, 6, 3, 5), (4,)):
        at = [lax.rem(kv + offset, kv_size) for offset in group]
        for offset, slot in zip(group, at):
            if offset:
                query_copy(offset, slot, offset).wait_recv()
        scores = [
            lax.dot_general(
                r3[slot, :GROUP, :],
                turned_keys[slot],
                (((1,), (0,)), ((), ())),
                preferred_element_type=F32,
            )
            * score_scale
            for slot in at
        ]
        results = []
        for slot, score in zip(at, scores):
            limit = len_smem[pool_smem[row * slots + slot]]
            score = jnp.where(position < limit, score, FLOOR)
            peak = jnp.maximum(jnp.max(score, axis=1, keepdims=True), 0.1 * FLOOR)
            weights = jnp.exp(score - peak)
            total = jnp.sum(weights, axis=1, keepdims=True)
            product = jnp.dot(weights.astype(BF16), values_v[slot], preferred_element_type=F32)
            results.append((product, jnp.where(lane == 0, peak, total)))
        for offset, slot, (product, stats) in zip(group, at, results):
            place = slot // quarter * kv_size + kv
            s4[slot, :GROUP] = product
            s4[slot, GROUP:] = stats
            for target in ((offset + 2) % kv_size, (offset + 2 + quarter) % kv_size):
                if target == 0:
                    r4[place] = s4[slot]
                else:
                    pltpu.make_async_remote_copy(
                        src_ref=s4.at[slot],
                        dst_ref=r4.at[place],
                        send_sem=send_sems.at[3],
                        recv_sem=recv_sems.at[3],
                        device_id={"kv": lax.rem(kv + target, kv_size)},
                        device_id_type=MESH,
                    ).start()

    @pl.when(jnp.logical_not(owns_fresh))
    def _():
        whole(10, rp).wait_recv()

    fresh = rp[...].astype(F32)
    fresh_keys, fresh_values = fresh[:slots], fresh[slots:]
    new_keys[...] = fresh_keys.astype(BF16)
    new_values[...] = fresh_values.astype(BF16)
    fresh = []
    for which in range(2):
        slot = lax.rem(kv + 2, quarter) + quarter * which
        this_slot = iota((slots, HEAD), 0) == slot
        fresh_key = jnp.sum(jnp.where(this_slot, fresh_keys, 0.0), axis=0, keepdims=True)
        fresh_value = jnp.sum(jnp.where(this_slot, fresh_values, 0.0), axis=0, keepdims=True)
        fresh_query = r3[slot].astype(F32)[:GROUP]
        fresh_score = jnp.sum(fresh_query * fresh_key, axis=1, keepdims=True) * score_scale
        fresh.append((fresh_score, fresh_value))
    arrived(3)
    mixed = []
    for which, (fresh_score, fresh_value) in enumerate(fresh):
        parts = r4[which * kv_size : (which + 1) * kv_size]
        peaks = [parts[source, GROUP:, 0:1] for source in range(slots)]
        joint = fresh_score
        for peak in peaks:
            joint = jnp.maximum(joint, peak)
        fresh_weight = jnp.exp(fresh_score - joint)
        total = fresh_weight
        numer = fresh_weight.astype(BF16).astype(F32) * fresh_value
        for source in range(slots):
            fade = jnp.exp(peaks[source] - joint)
            total = total + parts[source, GROUP:, 1:2] * fade
            numer = numer + parts[source, :GROUP] * fade
        mixed.append(numer / total)
    mixed = jnp.concatenate(mixed, axis=0).astype(BF16)

    pair = row * quarter + lax.rem(kv + 2, quarter)
    s5[...] = mixed
    r5[pair] = mixed
    for kv_step, row_step in (
        (2, 2), (2, 1), (2, 3), (7, 2), (1, 2), (2, 0), (7, 1), (7, 3),
        (1, 1), (1, 3), (0, 2), (7, 0), (1, 0), (0, 1), (0, 3),
    ):
        pltpu.make_async_remote_copy(
            src_ref=s5,
            dst_ref=r5.at[pair],
            send_sem=send_sems.at[4],
            recv_sem=recv_sems.at[4],
            device_id={
                "row": lax.rem(row + row_step, row_size),
                "kv": lax.rem(kv + kv_step, kv_size),
            },
            device_id_type=MESH,
        ).start()
    need("out")
    arrived(4)
    w8[...] = r5[...].astype(F32).reshape(w8.shape)
    mixed_all = jnp.concatenate(
        [w8[pl.ds(head, seqs, stride=8), :].astype(BF16) for head in range(GROUP)], axis=1
    )
    projected = jnp.dot(mixed_all, out_v[...], preferred_element_type=F32)

    half = seqs // 2
    half_rows = row_size // 2
    my_block = row // half_rows

    projected = projected.astype(BF16)
    for block, phase in enumerate((5, 11)):
        part = projected[block * half : (block + 1) * half]
        s6[block] = part
        r6[block, tp] = part
        send_tp(phase, s6.at[block], r6.at[block, tp])
    need("ffn", "gate", "up")
    ffn = ffn_gain[...].astype(F32).reshape(1, width)
    blank = jnp.zeros((half, HEAD), F32)
    chunks = gate_v.shape[1] // HEAD
    streams = []
    for block, phase in enumerate((5, 11)):
        arrived(phase)
        total = r6[block, 0].astype(F32)
        for source in range(1, tp_size):
            total = total + r6[block, source].astype(F32)
        rows = (stream_pairs[block * half : (block + 1) * half] + total).astype(BF16).astype(F32)
        streams.append(rows)
        square_column = jnp.broadcast_to(
            jnp.sum(rows * rows, axis=1, keepdims=True), (half, HEAD)
        )
        scaled = (rows * ffn).astype(BF16)

        gate = jnp.dot(scaled, gate_v[...], preferred_element_type=F32)
        up = jnp.dot(scaled, up_v[...], preferred_element_type=F32)
        base = block * half * 32
        for part in range(chunks):
            columns = slice(part * HEAD, (part + 1) * HEAD)
            w7[pl.ds(base + part, half, stride=32), :] = gate[:, columns]
            w7[pl.ds(base + part + 16, half, stride=32), :] = up[:, columns]
        high = square_column.astype(BF16).astype(F32)
        w7[pl.ds(base + 14, half, stride=32), :] = high
        w7[pl.ds(base + 15, half, stride=32), :] = square_column - high
        w7[pl.ds(base + 30, half, stride=32), :] = blank
        w7[pl.ds(base + 31, half, stride=32), :] = blank
        s7[base : base + half * 32, :] = w7[base : base + half * 32, :].astype(BF16)

        def send_partial(index, carry, block=block):
            other_row = block * half_rows + lax.rem(index, half_rows)
            other_kv = lax.rem(kv + far_first(index // half_rows, kv_size), kv_size)
            other = other_row * kv_size + other_kv

            @pl.when(other != me)
            def _():
                pltpu.make_async_remote_copy(
                    src_ref=s7.at[pl.ds(pl.multiple_of(other * 32, 32), 32), :],
                    dst_ref=r7.at[me],
                    send_sem=send_sems.at[6],
                    recv_sem=recv_sems.at[6],
                    device_id={"row": other_row, "kv": other_kv},
                    device_id_type=MESH,
                ).start()

            return carry

        lax.fori_loop(0, half, send_partial, 0)
    r7[me] = s7[pl.ds(pl.multiple_of(me * 32, 32), 32), :]
    need("down")
    drain(0, 1, 2, 3, 4)
    drain_fresh()
    arrived(6)
    sums = jnp.sum(r7[...].astype(F32), axis=0)
    scale = lax.rsqrt((sums[14:15] + sums[15:16]) / D + EPSILON)
    gate = sums[:16] * scale
    up = sums[16:] * scale
    activated = (gate / (1.0 + jnp.exp(-gate)) * up).astype(BF16)

    s8[...] = activated
    r8[me] = activated
    def share_activated(index, carry):
        other_row, other_kv = plane_partner(index)
        pltpu.make_async_remote_copy(
            src_ref=s8,
            dst_ref=r8.at[me],
            send_sem=send_sems.at[7],
            recv_sem=recv_sems.at[7 + 6 * my_block],
            device_id={"row": other_row, "kv": other_kv},
            device_id_type=MESH,
        ).start()
        return carry

    lax.fori_loop(0, plane - 1, share_activated, 0)
    drain(5, 11, 6)
    for block, phase in enumerate((8, 12)):

        @pl.when(my_block == block)
        def _(block=block):
            whole(7 + 6 * block, r8.at[pl.ds(0, half - 1)]).wait_recv()

        @pl.when(my_block != block)
        def _(block=block):
            whole(7 + 6 * block, r8.at[pl.ds(0, half)]).wait_recv()

        w8[...] = r8[block * half : (block + 1) * half].astype(F32).reshape(w8.shape)
        active = jnp.concatenate(
            [w8[pl.ds(part, half, stride=16), :].astype(BF16) for part in range(chunks)], axis=1
        )
        down = jnp.dot(active, down_v[...], preferred_element_type=F32).astype(BF16)

        s9[block] = down
        r9[block, tp] = down
        send_tp(phase, s9.at[block], r9.at[block, tp])
    results = []
    for block, phase in enumerate((8, 12)):
        arrived(phase)
        total = r9[block, 0].astype(F32)
        for source in range(1, tp_size):
            total = total + r9[block, source].astype(F32)
        results.append((streams[block] + total).astype(BF16))
    result = jnp.concatenate(results, axis=0)
    layer_out[...] = jnp.dot(to_seqs, result, preferred_element_type=F32).astype(BF16)
    drain(7, 8, 12)


def hand_out(result, keys, values, layer_out, new_keys, new_values, sems):
    copies = [
        pltpu.make_async_copy(result, layer_out, sems.at[0]),
        pltpu.make_async_copy(keys, new_keys, sems.at[1]),
        pltpu.make_async_copy(values, new_values, sems.at[2]),
    ]
    for copy in copies:
        copy.start()
    for copy in copies:
        copy.wait()


def local(
    sizes,
    tokens,
    attn_gain,
    w_qkv,
    w_out,
    ffn_gain,
    w_gate,
    w_up,
    w_down,
    cache_keys,
    cache_values,
    cache_len,
    pool_seq,
):
    tp_size, row_size, kv_size = sizes
    seqs, width = tokens.shape
    pair = np.arange(HEAD) % (HEAD // 2)
    frequency = (ROPE_BASE ** (-2.0 * pair / HEAD)).astype(np.float32).reshape(1, HEAD)
    plane = row_size * kv_size
    vmem = pl.BlockSpec(memory_space=pltpu.VMEM)
    hbm = pl.BlockSpec(memory_space=pltpu.HBM)
    scratch = [
        pltpu.VMEM((1, HEAD), F32),
        pltpu.SMEM(pool_seq.shape, jnp.int32),
        pltpu.SMEM(cache_len.shape, jnp.int32),
        pltpu.VMEM(tokens.shape, BF16),
        pltpu.VMEM(attn_gain.shape, BF16),
        pltpu.VMEM(ffn_gain.shape, BF16),
        pltpu.VMEM(w_qkv.shape, BF16),
        pltpu.VMEM(w_out.shape, BF16),
        pltpu.VMEM(w_gate.shape, BF16),
        pltpu.VMEM(w_up.shape, BF16),
        pltpu.VMEM(w_down.shape, BF16),
        pltpu.VMEM(cache_keys.shape, BF16),
        pltpu.VMEM(cache_values.shape, BF16),
        pltpu.VMEM((kv_size, HEAD, cache_keys.shape[1]), BF16),
        pltpu.VMEM((1, 1, HEAD), F32),
        pltpu.VMEM((plane, 1, HEAD), F32),
        pltpu.VMEM((plane * 8, HEAD), F32),
        pltpu.VMEM((plane, 8, HEAD), F32),
        pltpu.VMEM((row_size, 16, HEAD), BF16),
        pltpu.VMEM((plane, 16, HEAD), BF16),
        pltpu.VMEM((16, HEAD), BF16),
        pltpu.VMEM((kv_size, 16, HEAD), BF16),
        pltpu.VMEM((16, HEAD), BF16),
        pltpu.VMEM((16, HEAD), BF16),
        pltpu.VMEM((kv_size, 16, HEAD), F32),
        pltpu.VMEM((2 * kv_size, 16, HEAD), F32),
        pltpu.VMEM((16, HEAD), BF16),
        pltpu.VMEM((plane // 2, 16, HEAD), BF16),
        pltpu.VMEM((2, seqs // 2, width), BF16),
        pltpu.VMEM((2, tp_size, seqs // 2, width), BF16),
        pltpu.VMEM((plane * 32, HEAD), F32),
        pltpu.VMEM((plane * 32, HEAD), BF16),
        pltpu.VMEM((plane, 32, HEAD), BF16),
        pltpu.VMEM((16, HEAD), BF16),
        pltpu.VMEM((plane, 16, HEAD), BF16),
        pltpu.VMEM((plane * 8, HEAD), F32),
        pltpu.VMEM((2, seqs // 2, width), BF16),
        pltpu.VMEM((2, tp_size, seqs // 2, width), BF16),
        pltpu.SemaphoreType.DMA((13,)),
        pltpu.SemaphoreType.DMA((14,)),
        pltpu.SemaphoreType.DMA((14,)),
        pltpu.SemaphoreType.DMA((kv_size,)),
    ]
    result, keys, values = pl.pallas_call(
        functools.partial(kernel, tp_size, row_size, kv_size),
        out_shape=(
            jax.ShapeDtypeStruct((seqs, width), BF16),
            jax.ShapeDtypeStruct((kv_size, HEAD), BF16),
            jax.ShapeDtypeStruct((kv_size, HEAD), BF16),
        ),
        in_specs=[hbm] * 13,
        out_specs=(vmem, vmem, vmem),
        scratch_shapes=scratch,
        compiler_params=pltpu.CompilerParams(
            collective_id=0, has_side_effects=True, vmem_limit_bytes=24 * 1024 * 1024
        ),
    )(
        *(
            pltpu.with_memory_space_constraint(part, pltpu.HBM)
            for part in (
                frequency,
                pool_seq,
                cache_len,
                tokens,
                attn_gain,
                ffn_gain,
                w_qkv,
                w_out,
                w_gate,
                w_up,
                w_down,
                cache_keys,
                cache_values,
            )
        )
    )
    return pl.pallas_call(
        hand_out,
        out_shape=(
            jax.ShapeDtypeStruct((seqs, width), BF16),
            jax.ShapeDtypeStruct((kv_size, HEAD), BF16),
            jax.ShapeDtypeStruct((kv_size, HEAD), BF16),
        ),
        in_specs=[vmem] * 3,
        out_specs=(hbm, hbm, hbm),
        scratch_shapes=[pltpu.SemaphoreType.DMA((3,))],
    )(*(pltpu.with_memory_space_constraint(part, pltpu.VMEM) for part in (result, keys, values)))


def solution(mesh):
    sizes = (mesh.shape["tp"], mesh.shape["row"], mesh.shape["kv"])
    return jax.shard_map(
        functools.partial(local, sizes),
        mesh=mesh,
        in_specs=(
            P(None, ("row", "kv")),
            P(("row", "kv")),
            P(("row", "kv"), "tp"),
            P("tp", ("row", "kv")),
            P(("row", "kv")),
            P(("row", "kv"), "tp"),
            P(("row", "kv"), "tp"),
            P("tp", ("row", "kv")),
            P("row", "kv", "tp"),
            P("row", "kv", "tp"),
            P(),
            P(),
        ),
        out_specs=(P(None, ("row", "kv")), P("row", "tp"), P("row", "tp")),
        check_vma=False,
    )
```
